512 devices in a mesh: cell: 64 (over z_lo, x, core), gene: 8 (over y, z_hi).
Axes of the slice: x: 4, y: 4, z: 16 (z_hi: 2, z_lo: 8; z = z_hi * 8 + z_lo), core: 2. Of those that a mesh axis runs over, the one named last changes fastest.
Arguments:
- counts: bfloat16 [61440, 16384], P('cell', 'gene'), as said below
- w_factor: float32 [61440, 128], P('cell'), may hold values from 0.004 to 2, as said below
- h_factor: float32 [128, 16384], P('cell', 'gene'), may hold values from 0.03 to 0.3, as said below
Outputs:
- w_updated: float32 [61440, 128], P('cell')
- h_updated: float32 [128, 16384], P('cell', 'gene')
The draws below stay inside these ranges and needn't reach their ends.
Inputs may be any that keep to these rules, and one draw needn't show every extreme that they name: `counts`: nonnegative whole numbers. `w_factor`: positive. `h_factor`: positive.
All inputs are finite; a program needn't handle non-finite values.
Results may differ from the reference program's by a relative error of at most 0.00092.
Values may be sent and summed in bfloat16 or wider, within the bound.
A program may use at most 64 MiB of HBM per device.

```python
import jax
import jax.numpy as jnp
from jax import lax

K = 128
GENES = 16384
CELL_DEV = 960
CELLS = 61440


def log_spread(key, shape, lower, upper):
    span = jnp.log(upper) - jnp.log(lower)
    return jnp.exp(jnp.log(lower) + span * jax.random.uniform(key, shape, jnp.float32))


def factor_pair(key):
    keys = jax.random.split(jax.random.fold_in(key, 101), 3)
    lower, upper, lift = (0.005, 0.05, 40.0)
    share = 4.0 / K
    base = log_spread(keys[0], (CELLS, K), lower, upper)
    raised = jnp.where(jax.random.uniform(keys[1], (CELLS, K), jnp.float32) < share, lift, 1.0)
    w_values = base * raised
    h_values = log_spread(keys[2], (K, GENES), 0.03, 0.3)
    return (w_values, h_values)


def draw_w_factor(key, part):
    w_values, h_values = factor_pair(key)
    return w_values


def draw_h_factor(key, part):
    w_values, h_values = factor_pair(key)
    return h_values


def draw_counts(key, part):
    w_values, h_values = factor_pair(key)
    keys = jax.random.split(jax.random.fold_in(key, 11), 4)
    tilt = log_spread(keys[0], (K, GENES), 0.3, 3.0)
    depth = log_spread(keys[1], (CELLS, 1), 0.3, 3.0)
    gene_scale = log_spread(keys[2], (1, GENES), 0.3, 3.0)
    expected = jnp.dot(w_values, h_values * tilt, precision=lax.Precision.HIGHEST)
    noise = jax.random.uniform(keys[3], (CELLS, GENES), jnp.float32)
    values = jnp.floor(3.0 * depth * gene_scale * noise * expected)
    values = jnp.minimum(values, 200.0)
    return values.astype(jnp.bfloat16)


def setup_inputs(seed: int = 0) -> dict:
    streams_of = jax.random.split(jax.random.key(seed), 4)
    counts = draw_counts(jax.random.fold_in(streams_of[3], 71), 0)
    w_factor = draw_w_factor(jax.random.fold_in(streams_of[3], 71), 0)
    h_factor = draw_h_factor(jax.random.fold_in(streams_of[3], 71), 0)
    return {"counts": counts, "w_factor": w_factor, "h_factor": h_factor}


def reference(counts, w_factor, h_factor):
    blocks = CELLS // CELL_DEV
    count_blocks = counts.reshape(blocks, CELL_DEV, GENES)
    w_blocks = w_factor.reshape(blocks, CELL_DEV, K)
    h_copy = h_factor.astype(jnp.bfloat16)

    def h_step(running, pair):
        block_counts, block_w = pair
        w_copy = block_w.astype(jnp.bfloat16)
        modeled = jnp.dot(w_copy, h_copy, preferred_element_type=jnp.float32)
        quotient = (block_counts.astype(jnp.float32) / modeled).astype(jnp.bfloat16)
        term = lax.dot_general(w_copy, quotient, (((0,), (0,)), ((), ())), preferred_element_type=jnp.float32)
        return running + term, None

    h_numerator, _ = lax.scan(h_step, jnp.zeros((K, GENES), jnp.float32), (count_blocks, w_blocks))
    w_totals = jnp.sum(w_factor, axis=0)
    h_updated = h_factor * h_numerator / w_totals[:, None]
    h_new_copy = h_updated.astype(jnp.bfloat16)
    h_totals = jnp.sum(h_new_copy.astype(jnp.float32), axis=1)

    def w_step(carry, pair):
        block_counts, block_w = pair
        w_copy = block_w.astype(jnp.bfloat16)
        modeled = jnp.dot(w_copy, h_new_copy, preferred_element_type=jnp.float32)
        quotient = (block_counts.astype(jnp.float32) / modeled).astype(jnp.bfloat16)
        numerator = lax.dot_general(quotient, h_new_copy, (((1,), (1,)), ((), ())), preferred_element_type=jnp.float32)
        return carry, block_w * numerator / h_totals[None, :]

    _, w_new = lax.scan(w_step, jnp.zeros((), jnp.float32), (count_blocks, w_blocks))
    return w_new.reshape(CELLS, K), h_updated
```

```python
import jax
import jax.numpy as jnp
from jax import lax
from jax.experimental import pallas as pl
from jax.experimental.pallas import tpu as pltpu
from jax.sharding import PartitionSpec as P

MESH = pl.DeviceIdType.MESH
BF = jnp.bfloat16
F32 = jnp.float32
NC = 2
CH = 2048 // NC
ZG = CH // 8
ROWS = 240


def iota(shape, dim):
    return lax.broadcasted_iota(jnp.int32, shape, dim)


def natural(i):
    return ((i % 16) // 2) * 16 + ((i // 16) % 4) * 4 + (i // 64) * 2 + i % 2


def spread(tile, rows, columns):
    wide = jnp.concatenate([tile] * (columns // 128), axis=1) if columns > 128 else tile
    return jnp.concatenate([wide] * (rows // 8), axis=0) if rows > 8 else wide


def scale_of(value):
    rows, columns = value.shape
    top = jnp.full((8, 128), 1e-30, F32)
    for r in range(0, rows, 8):
        for c in range(0, columns, 128):
            top = jnp.maximum(top, value[r : r + 8, c : c + 128])
    return top.astype(BF)


def encode(value, scale):
    rows, columns = value.shape
    share = value * spread(32768.0 / scale.astype(F32), rows, columns)
    square = share * share
    fourth = square * square
    return (fourth * fourth).astype(BF)


def decode(code, scale16):
    rows, columns = code.shape
    unit = scale16[0:8, :].astype(F32) * (1.0 / 32768.0)
    root = jnp.sqrt(jnp.sqrt(jnp.sqrt(code.astype(F32))))
    return root * spread(unit, rows, columns)


def twice(scale):
    wide = scale.astype(F32)
    return jnp.concatenate([wide, wide], axis=0).astype(BF)


def kernel(
    cnt_hbm, w_hbm, h_in, w_out, h_out,
    cnt, wf, wp, wt, quo,
    hown, ha, hx32, hmat, fm, fr, h16, tx, tc,
    num, numr, bs, bx, bxr, tz, bz, bzr, hu, ho, outr, hmat2, hn, ht,
    wn, dy, dyr, dz, zr, da,
    ls, as_, ar, fs, frs, txs, txr, tcs, tcr,
    xs, xr, cs, cr, ns, nr, bxs, bxrs, bzs, bzrs, cz, czr, os_, ors, hts, htr,
    dys, dyrs, dzs, dzr, das, dar,
):
    c = lax.axis_index("cell")
    g = lax.axis_index("gene")
    z, x, k = c // 8, (c // 2) % 4, c % 2
    y, zh = g // 2, g % 2
    slot = k * 4 + x

    def at_z(d):
        return (((z + d) % 8) * 8 + x * 2 + k, g)

    def at_x(d):
        return (z * 8 + ((x + d) % 4) * 2 + k, g)

    def at_y(d):
        return (c, ((y + d) % 4) * 2 + zh)

    at_core = (z * 8 + x * 2 + (1 - k), g)
    at_zh = (c, y * 2 + (1 - zh))
    sent = []

    def send(src, dst, ssem, rsem, device):
        copy = pltpu.make_async_remote_copy(
            src_ref=src, dst_ref=dst, send_sem=ssem, recv_sem=rsem, device_id=device, device_id_type=MESH
        )
        copy.start()
        sent.append(copy)
        return copy

    load_cnt = pltpu.make_async_copy(cnt_hbm, cnt, ls.at[0])
    load_w = pltpu.make_async_copy(w_hbm, wf, ls.at[1])
    load_w.start()
    load_cnt.start()

    barrier = pltpu.get_barrier_semaphore()
    friends = [at_z(d) for d in range(1, 8)] + [at_x(d) for d in range(1, 4)] + [at_core]
    friends += [(c, (g + d) % 8) for d in range(1, 8)]
    for friend in friends:
        pl.semaphore_signal(barrier, inc=1, device_id=friend, device_id_type=MESH)

    h_own = h_in[...]
    hown[...] = h_own.astype(BF)
    load_w.wait()
    w_all = wf[...]
    w_sum = jnp.sum(w_all, axis=0, keepdims=True)
    fm[...] = jnp.zeros_like(fm)
    for zz in range(8):
        for n in range(NC):
            base = n * CH + zz * ZG
            fm[zz, 2 * n : 2 * n + 2, :] = h_own[:, base : base + ZG]
        fm[zz, 4:5, :] = w_sum
    pl.semaphore_wait(barrier, len(friends))

    got_a = []
    got_f = []
    for d in range(1, 8):
        got_a.append(send(hown, ha.at[z], as_.at[d - 1], ar.at[d - 1], at_z(d)))
    for d in range(1, 8):
        got_f.append(send(fm.at[(z + d) % 8], fr.at[z], fs.at[d - 1], frs.at[d - 1], at_z(d)))
    ha[z] = hown[...]
    fr[z] = fm[z]

    w_copy = w_all.astype(BF)
    pick = (iota((128, 128), 0) == natural(iota((128, 128), 1))).astype(F32).astype(BF)
    pick_t = (natural(iota((128, 128), 0)) == iota((128, 128), 1)).astype(F32).astype(BF)
    wp[...] = jnp.dot(w_copy, pick, preferred_element_type=F32).astype(BF)
    wt[...] = lax.dot_general(
        pick_t, w_copy, (((1,), (1,)), ((), ())), preferred_element_type=F32
    ).astype(BF)

    for copy in got_a:
        copy.wait_recv()
    for zz in range(8):
        hx32[2 * zz : 2 * zz + 2, :] = ha[zz].astype(F32)
    hmat[slot] = hx32[...].astype(BF)

    def fan_out(buf, phase, n):
        cols = pl.ds(n * CH, CH)
        mine = buf.at[slot, :, cols]
        got_x = [
            send(mine, mine, xs.at[phase, n, d - 1], xr.at[phase, n, d - 1], at_x(d)) for d in range(1, 4)
        ]
        got_c = [send(mine, mine, cs.at[phase, n, 0], cr.at[phase, n, 0], at_core)]
        return got_x, got_c

    def fan_on(buf, phase, n, got):
        cols = pl.ds(n * CH, CH)
        for d in (1, 3, 2):
            got[0][d - 1].wait_recv()
            piece = buf.at[k * 4 + (x + 4 - d) % 4, :, cols]
            got[1].append(send(piece, piece, cs.at[phase, n, d], cr.at[phase, n, d], at_core))

    def fan_in(got):
        for copy in got[1]:
            copy.wait_recv()

    got = [fan_out(hmat, 0, n) for n in range(NC)]

    for copy in got_f:
        copy.wait_recv()
    tot = jnp.zeros((1, 128), F32)
    for zz in range(8):
        tot = tot + fr[zz, 4:5, :]
        for n in range(NC):
            h16[n, 2 * zz : 2 * zz + 2, :] = fr[zz, 2 * n : 2 * n + 2, :]
    tx[x] = jnp.broadcast_to(tot, (8, 128))
    got_t = [send(tx.at[x], tx.at[x], txs.at[d - 1], txr.at[d - 1], at_x(d)) for d in range(1, 4)]
    load_cnt.wait()
    for n in range(NC):
        fan_on(hmat, 0, n, got[n])
    for copy in got_t:
        copy.wait_recv()
    tc[k] = tx[0] + tx[1] + tx[2] + tx[3]
    got_tc = send(tc.at[k], tc.at[k], tcs.at[0], tcr.at[0], at_core)

    got_n = []
    for n in range(NC):
        cols = slice(n * CH, (n + 1) * CH)
        fan_in(got[n])
        h_chunk = hmat[:, :, cols].reshape(128, CH)
        for i in range(8):
            rows = slice(i * 120, (i + 1) * 120)
            modeled = jnp.dot(wp[rows, :], h_chunk, preferred_element_type=F32)
            counts = cnt[rows, cols].astype(F32)
            quo[rows, :] = (counts * pltpu.reciprocal(modeled, approx=True)).astype(BF)
        part = jnp.dot(wt[...], quo[...], preferred_element_type=F32)
        num[n, 0] = part[0:64, :]
        num[n, 1] = part[64:128, :]
        got_n.append(send(num.at[n, 1 - k], numr.at[n], ns.at[n], nr.at[n], at_core))
    got_tc.wait_recv()
    w_totals = tc[0][0:1, :] + tc[1][0:1, :]
    places = iota((16, 128), 0)
    own = (places // 2) * 16 + x * 4 + k * 2 + places % 2 == iota((16, 128), 1)
    w_column = jnp.sum(jnp.where(own, w_totals, 0.0), axis=1, keepdims=True)

    got_bx = []
    for n in range(NC):
        got_n[n].wait_recv()
        both = num[n, k] + numr[n]
        bs[n] = both.reshape(4, 16, CH)
        scale = scale_of(both)
        code = encode(both, scale)
        scale2 = twice(scale)
        for s in range(4):
            bx[n, s, :, 0:CH] = code[16 * s : 16 * s + 16, :]
            bx[n, s, :, CH : CH + 128] = scale2
        got_bx.append([
            send(bx.at[n, (x + d) % 4], bxr.at[n, d - 1], bxs.at[n, d - 1], bxrs.at[n, d - 1], at_x(d))
            for d in range(1, 4)
        ])
    got_bz = []
    for n in range(NC):
        total = bs[n, x]
        for d in (1, 3, 2):
            got_bx[n][d - 1].wait_recv()
            total = total + decode(bxr[n, d - 1, :, 0:CH], bxr[n, d - 1, :, CH : CH + 128])
        scale = scale_of(total)
        code = encode(total, scale)
        scale2 = twice(scale)
        for s in range(8):
            tz[n, s] = total[:, s * ZG : (s + 1) * ZG]
            bz[n, s, :, 0:ZG] = code[:, s * ZG : (s + 1) * ZG]
            bz[n, s, :, ZG : ZG + 128] = scale2
        got_bz.append([
            send(bz.at[n, (z + d) % 8], bzr.at[n, d - 1], bzs.at[n, d - 1], bzrs.at[n, d - 1], at_z(d))
            for d in range(1, 8)
        ])
    got_cz = []
    got_o = []
    for n in range(NC):
        total = tz[n, z]
        for d in range(1, 8):
            got_bz[n][d - 1].wait_recv()
            total = total + decode(bzr[n, d - 1, :, 0:ZG], bzr[n, d - 1, :, ZG : ZG + 128])
        updated = h16[n] * total / w_column
        hu[n] = updated.astype(BF)
        cols = pl.ds(pl.multiple_of(n * CH + z * ZG, ZG), ZG)
        hmat2[slot, :, cols] = hu[n]
        got_cz.append([
            send(hu.at[n], hmat2.at[slot, :, cols], cz.at[n, d - 1], czr.at[n, d - 1], at_z(d))
            for d in range(1, 8)
        ])
        for zz in range(8):
            ho[n, zz] = updated[2 * zz : 2 * zz + 2, :]
    for n in range(NC):
        cols = pl.ds(pl.multiple_of(n * CH + z * ZG, ZG), ZG)
        outr[:, cols] = ho[n, z]
        for d in range(1, 8):
            got_o.append(
                send(ho.at[n, (z + d) % 8], outr.at[:, cols], os_.at[n, d - 1], ors.at[n, d - 1], at_z(d))
            )

    got = []
    for n in range(NC):
        for copy in got_cz[n]:
            copy.wait_recv()
        got.append(fan_out(hmat2, 1, n))
    for n in range(NC):
        fan_on(hmat2, 1, n, got[n])
    for n in range(NC):
        fan_in(got[n])
    h_all = hmat2[...].reshape(128, 2048)
    hn[...] = jnp.dot(pick, h_all, preferred_element_type=F32).astype(BF)
    ht[g] = lax.dot_general(
        jnp.ones((8, 2048), BF), hn[...], (((1,), (1,)), ((), ())), preferred_element_type=F32
    )
    got_h = [
        send(ht.at[g], ht.at[g], hts.at[d - 1], htr.at[d - 1], (c, (g + d) % 8)) for d in range(1, 8)
    ]

    got_y = {}
    for d in (2, 1, 3, 0):
        first_row = ((y + d) % 4) * ROWS
        rows = pl.ds(pl.multiple_of(first_row, 16), ROWS)
        acc = None
        for j in range(4):
            cols = slice(j * 512, (j + 1) * 512)
            modeled = jnp.dot(
                wp[rows, :], hmat2[:, :, cols].reshape(128, 512), preferred_element_type=F32
            )
            counts = cnt[rows, cols].astype(F32)
            quotient = (counts * pltpu.reciprocal(modeled, approx=True)).astype(BF)
            term = lax.dot_general(
                quotient, hn[:, cols], (((1,), (1,)), ((), ())), preferred_element_type=F32
            )
            acc = term if acc is None else acc + term
        if d:
            scale = scale_of(acc)
            dy[d - 1, 0:ROWS, :] = encode(acc, scale)
            dy[d - 1, ROWS : ROWS + 16, :] = twice(scale)
            got_y[d] = send(dy.at[d - 1], dyr.at[d - 1], dys.at[d - 1], dyrs.at[d - 1], at_y(d))
        else:
            wn[...] = acc
    total = wn[...]
    for d in (2, 1, 3):
        got_y[d].wait_recv()
        total = total + decode(dyr[d - 1, 0:ROWS, :], dyr[d - 1, ROWS : ROWS + 16, :])
    scale = scale_of(total)
    dz[0:ROWS, :] = encode(total, scale)
    dz[ROWS : ROWS + 16, :] = twice(scale)
    got_z = send(dz, zr, dzs.at[0], dzr.at[0], at_zh)

    for copy in got_h:
        copy.wait_recv()
    h_totals = ht[0]
    for i in range(1, 8):
        h_totals = h_totals + ht[i]
    for copy in got_o:
        copy.wait_recv()
    h_out[...] = outr[...]

    got_z.wait_recv()
    total = decode(dz[0:ROWS, :], dz[ROWS : ROWS + 16, :]) + decode(zr[0:ROWS, :], zr[ROWS : ROWS + 16, :])
    scale = scale_of(total)
    da[y, 0:ROWS, :] = encode(total, scale)
    da[y, ROWS : ROWS + 16, :] = twice(scale)
    got_w = [send(da.at[y], da.at[y], das.at[d - 1], dar.at[d - 1], at_y(d)) for d in range(1, 4)]
    inverse = spread(1.0 / h_totals, ROWS, 128)
    for d in (0, 1, 3, 2):
        if d:
            got_w[d - 1].wait_recv()
        p = (y + 4 - d) % 4
        rows = pl.ds(pl.multiple_of(p * ROWS, 16), ROWS)
        w_out[rows, :] = wf[rows, :] * (decode(da[p, 0:ROWS, :], da[p, ROWS : ROWS + 16, :]) * inverse)
    for copy in sent:
        copy.wait_send()


def per_device(counts, w_factor, h_factor):
    vmem = pltpu.VMEM
    dma = pltpu.SemaphoreType.DMA
    anywhere = pl.BlockSpec(memory_space=pl.ANY)
    local = pl.BlockSpec(memory_space=pltpu.VMEM)
    return pl.pallas_call(
        kernel,
        out_shape=(
            jax.ShapeDtypeStruct((960, 128), F32),
            jax.ShapeDtypeStruct((2, 2048), F32),
        ),
        in_specs=[anywhere, anywhere, local],
        out_specs=(local, local),
        scratch_shapes=[
            vmem((960, 2048), BF), vmem((960, 128), F32), vmem((960, 128), BF), vmem((128, 960), BF),
            vmem((960, CH), BF),
            vmem((2, 2048), BF), vmem((8, 2, 2048), BF), vmem((16, 2048), F32), vmem((8, 16, 2048), BF),
            vmem((8, 8, 128), F32), vmem((8, 8, 128), F32), vmem((NC, 16, ZG), F32),
            vmem((4, 8, 128), F32), vmem((2, 8, 128), F32),
            vmem((NC, 2, 64, CH), F32), vmem((NC, 64, CH), F32), vmem((NC, 4, 16, CH), F32),
            vmem((NC, 4, 16, CH + 128), BF), vmem((NC, 3, 16, CH + 128), BF),
            vmem((NC, 8, 16, ZG), F32), vmem((NC, 8, 16, ZG + 128), BF), vmem((NC, 7, 16, ZG + 128), BF),
            vmem((NC, 16, ZG), BF), vmem((NC, 8, 2, ZG), F32), vmem((2, 2048), F32),
            vmem((8, 16, 2048), BF), vmem((128, 2048), BF), vmem((8, 8, 128), F32),
            vmem((ROWS, 128), F32), vmem((3, ROWS + 16, 128), BF), vmem((3, ROWS + 16, 128), BF),
            vmem((ROWS + 16, 128), BF), vmem((ROWS + 16, 128), BF), vmem((4, ROWS + 16, 128), BF),
            dma((2,)), dma((7,)), dma((7,)), dma((7,)), dma((7,)), dma((3,)), dma((3,)), dma((1,)), dma((1,)),
            dma((2, NC, 3)), dma((2, NC, 3)), dma((2, NC, 4)), dma((2, NC, 4)), dma((NC,)), dma((NC,)),
            dma((NC, 3)), dma((NC, 3)), dma((NC, 7)), dma((NC, 7)), dma((NC, 7)), dma((NC, 7)),
            dma((NC, 7)), dma((NC, 7)), dma((7,)), dma((7,)),
            dma((3,)), dma((3,)), dma((1,)), dma((1,)), dma((3,)), dma((3,)),
        ],
        compiler_params=pltpu.CompilerParams(
            collective_id=0, has_side_effects=True, vmem_limit_bytes=48 * 1024 * 1024
        ),
        name="nmf_update",
    )(counts, w_factor, h_factor)


def solution(mesh):
    in_specs = (P("cell", "gene"), P("cell", None), P("cell", "gene"))
    out_specs = (P("cell", None), P("cell", "gene"))
    return jax.shard_map(
        per_device, mesh=mesh, in_specs=in_specs, out_specs=out_specs, check_vma=False
    )
```

```python
import jax
import jax.numpy as jnp
from jax import lax
from jax.experimental import pallas as pl
from jax.experimental.pallas import tpu as pltpu
from jax.sharding import PartitionSpec as P

MESH = pl.DeviceIdType.MESH
BF = jnp.bfloat16
F32 = jnp.float32
NC = 2
CH = 2048 // NC
ZG = CH // 8
ROWS = 240
STARTS, SIZES = (0, 128), (128, 112)
NEAR = (1, 2, 3, 4, 5, 6, 7)
FAR = (7, 6, 5, 4, 3, 2, 1)


def iota(shape, dim):
    return lax.broadcasted_iota(jnp.int32, shape, dim)


def natural(i):
    return ((i % 16) // 2) * 16 + ((i // 16) % 4) * 4 + (i // 64) * 2 + i % 2


def spread(tile, rows, columns):
    wide = jnp.concatenate([tile] * (columns // 128), axis=1) if columns > 128 else tile
    return jnp.concatenate([wide] * (rows // 8), axis=0) if rows > 8 else wide


def scale_of(value):
    rows, columns = value.shape
    top = jnp.full((8, 128), 1e-30, F32)
    for r in range(0, rows, 8):
        for c in range(0, columns, 128):
            top = jnp.maximum(top, value[r : r + 8, c : c + 128])
    return top.astype(BF)


def encode(value, scale):
    rows, columns = value.shape
    share = value * spread(32768.0 / scale.astype(F32), rows, columns)
    square = share * share
    fourth = square * square
    return (fourth * fourth).astype(BF)


def decode(code, scale16):
    rows, columns = code.shape
    unit = scale16[0:8, :].astype(F32) * (1.0 / 32768.0)
    root = jnp.sqrt(jnp.sqrt(jnp.sqrt(code.astype(F32))))
    return root * spread(unit, rows, columns)


def twice(scale):
    wide = scale.astype(F32)
    return jnp.concatenate([wide, wide], axis=0).astype(BF)


def kernel(
    cnt_hbm, w_hbm, h_hbm, w_out, h_out,
    cnt, wf, h_in, wp, wt, quo,
    hown, ha, hx32, hmat, fm, fr, h16, tx, tc,
    num, numr, bs, bx, bxr, tz, bz, bzr, hu, ho, outr, hmat2, hn, ht, hz,
    wn, dy, dyr, dz, zr, da,
    ls, as_, ar, fs, frs, txs, txr, tcs, tcr,
    xs, xr, cs, cr, ns, nr, bxs, bxrs, bzs, bzrs, cz, czr, os_, ors, hts, htr, hzs, hzr,
    dys, dyrs, dzs, dzr, das, dar,
):
    c = lax.axis_index("cell")
    g = lax.axis_index("gene")
    z, x, k = c // 8, (c // 2) % 4, c % 2
    y, zh = g // 2, g % 2
    slot = k * 4 + x

    turn = jnp.where(z < 4, 1, 7)

    def z_of(d):
        return (z + turn * d) % 8

    def at_z(d):
        return (z_of(d) * 8 + x * 2 + k, g)

    def at_x(d):
        return (z * 8 + ((x + d) % 4) * 2 + k, g)

    def at_y(d):
        return (c, ((y + d) % 4) * 2 + zh)

    def genes(n, owner):
        return pl.ds(pl.multiple_of(n * CH + owner * ZG, ZG), ZG)

    at_core = (z * 8 + x * 2 + (1 - k), g)
    at_zh = (c, y * 2 + (1 - zh))
    sent = []

    def remote(src, dst, ssem, rsem, device):
        return pltpu.make_async_remote_copy(
            src_ref=src, dst_ref=dst, send_sem=ssem, recv_sem=rsem, device_id=device, device_id_type=MESH
        )

    def due(copy):
        return copy

    def send(src, dst, ssem, rsem, device):
        copy = remote(src, dst, ssem, rsem, device)
        copy.start()
        sent.append(copy)
        return due(copy)

    def send_z(src, dst, ssem, rsem):
        for d in FAR:
            copy = remote(src(z_of(d)), dst(z), ssem.at[d], rsem.at[z], at_z(d))
            copy.start()
            sent.append(copy)
        return [
            due(remote(src(z_of(d)), dst(z_of(d)), ssem.at[d], rsem.at[z_of(d)], at_z(d))) for d in NEAR
        ]

    barrier = pltpu.get_barrier_semaphore()
    friends = [at_z(d) for d in FAR] + [at_x(d) for d in range(1, 4)] + [at_core]
    friends += [at_y(d) for d in range(1, 4)] + [at_zh]
    for friend in friends:
        pl.semaphore_signal(barrier, inc=1, device_id=friend, device_id_type=MESH)

    load_h = pltpu.make_async_copy(h_hbm, h_in, ls.at[2])
    load_w = pltpu.make_async_copy(w_hbm, wf, ls.at[1])
    load_cnt = pltpu.make_async_copy(cnt_hbm, cnt, ls.at[0])
    load_h.start()
    load_w.start()
    load_cnt.start()
    load_h.wait()
    hown[...] = h_in[...].astype(BF)
    pl.semaphore_wait(barrier, len(friends))

    got_a = send_z(lambda s: hown, lambda s: ha.at[s], as_, ar)
    ha[z] = hown[...]

    load_w.wait()
    w_all = wf[...]
    w_sum = jnp.sum(w_all, axis=0, keepdims=True)
    h_own = h_in[...]
    for zz in range(8):
        for n in range(NC):
            base = n * CH + zz * ZG
            fm[zz, 2 * n : 2 * n + 2, :] = h_own[:, base : base + ZG]
        fm[zz, 4:5, :] = w_sum
    got_f = send_z(lambda s: fm.at[s], lambda s: fr.at[s], fs, frs)
    fr[z] = fm[z]
    w_copy = w_all.astype(BF)
    pick = (iota((128, 128), 0) == natural(iota((128, 128), 1))).astype(F32).astype(BF)
    pick_t = (natural(iota((128, 128), 0)) == iota((128, 128), 1)).astype(F32).astype(BF)
    wp[...] = jnp.dot(w_copy, pick, preferred_element_type=F32).astype(BF)
    wt[...] = lax.dot_general(
        pick_t, w_copy, (((1,), (1,)), ((), ())), preferred_element_type=F32
    ).astype(BF)

    for copy in got_a:
        copy.wait_recv()
    for zz in range(8):
        hx32[2 * zz : 2 * zz + 2, :] = ha[zz].astype(F32)
    hmat[slot] = hx32[...].astype(BF)

    def fan_out(buf, phase, n):
        cols = pl.ds(n * CH, CH)
        mine = buf.at[slot, :, cols]
        got_x = {d: send(mine, mine, xs.at[phase, n, d - 1], xr.at[phase, n, d - 1], at_x(d)) for d in (2, 1, 3)}
        got_c = [send(mine, mine, cs.at[phase, n, 0], cr.at[phase, n, 0], at_core)]
        return got_x, got_c

    def fan_on(buf, phase, n, got):
        cols = pl.ds(n * CH, CH)
        for d in (1, 3, 2):
            got[0][d].wait_recv()
            piece = buf.at[k * 4 + (x + 4 - d) % 4, :, cols]
            got[1].append(send(piece, piece, cs.at[phase, n, d], cr.at[phase, n, d], at_core))

    def fan_in(got):
        for copy in got[1]:
            copy.wait_recv()

    def quotients(n, first, last):
        cols = slice(n * CH, (n + 1) * CH)
        h_chunk = hmat[:, :, cols].reshape(128, CH)
        for i in range(first, last):
            rows = slice(i * 120, (i + 1) * 120)
            modeled = jnp.dot(wp[rows, :], h_chunk, preferred_element_type=F32)
            counts = cnt[rows, cols].astype(F32)
            quo[rows, :] = (counts * pltpu.reciprocal(modeled, approx=True)).astype(BF)

    def numerator(n):
        part = jnp.dot(wt[...], quo[...], preferred_element_type=F32)
        num[n, 0] = part[0:64, :]
        num[n, 1] = part[64:128, :]
        return send(num.at[n, 1 - k], numr.at[n], ns.at[n], nr.at[n], at_core)

    def sum_core(n, got):
        got.wait_recv()
        both = num[n, k] + numr[n]
        bs[n] = both.reshape(4, 16, CH)
        scale = scale_of(both)
        code = encode(both, scale)
        scale2 = twice(scale)
        for s in range(4):
            bx[n, s, :, 0:CH] = code[16 * s : 16 * s + 16, :]
            bx[n, s, :, CH : CH + 128] = scale2
        return {
            d: send(bx.at[n, (x + d) % 4], bxr.at[n, d - 1], bxs.at[n, d - 1], bxrs.at[n, d - 1], at_x(d))
            for d in (2, 1, 3)
        }

    def sum_x(n, got):
        total = bs[n, x]
        for d in (1, 3, 2):
            got[d].wait_recv()
            total = total + decode(bxr[n, d - 1, :, 0:CH], bxr[n, d - 1, :, CH : CH + 128])
        scale = scale_of(total)
        code = encode(total, scale)
        scale2 = twice(scale)
        for s in range(8):
            tz[n, s] = total[:, s * ZG : (s + 1) * ZG]
            bz[n, s, :, 0:ZG] = code[:, s * ZG : (s + 1) * ZG]
            bz[n, s, :, ZG : ZG + 128] = scale2
        return send_z(lambda s: bz.at[n, s], lambda s: bzr.at[n, s], bzs.at[n], bzrs.at[n])

    def sum_z(n, got):
        total = tz[n, z]
        for d in NEAR:
            s = z_of(d)
            got[d - 1].wait_recv()
            total = total + decode(bzr[n, s, :, 0:ZG], bzr[n, s, :, ZG : ZG + 128])
        updated = h16[n] * total / w_column
        hu[n] = updated.astype(BF)
        hmat2[slot, :, genes(n, z)] = hu[n]
        copies = send_z(lambda s: hu.at[n], lambda s: hmat2.at[slot, :, genes(n, s)], cz.at[n], czr.at[n])
        for zz in range(8):
            ho[n, zz] = updated[2 * zz : 2 * zz + 2, :]
        return copies

    got = [fan_out(hmat, 0, n) for n in range(NC)]

    for copy in got_f:
        copy.wait_recv()
    tot = jnp.zeros((1, 128), F32)
    for zz in range(8):
        tot = tot + fr[zz, 4:5, :]
        for n in range(NC):
            h16[n, 2 * zz : 2 * zz + 2, :] = fr[zz, 2 * n : 2 * n + 2, :]
    tx[x] = jnp.broadcast_to(tot, (8, 128))
    got_t = [send(tx.at[x], tx.at[x], txs.at[d - 1], txr.at[d - 1], at_x(d)) for d in (2, 1, 3)]
    load_cnt.wait()

    fan_on(hmat, 0, 0, got[0])
    fan_in(got[0])
    quotients(0, 0, 4)
    fan_on(hmat, 0, 1, got[1])
    quotients(0, 4, 8)
    got_n = [numerator(0)]
    fan_in(got[1])
    quotients(1, 0, 4)
    got_bx = [sum_core(0, got_n[0])]
    quotients(1, 4, 8)
    got_n.append(numerator(1))
    for copy in got_t:
        copy.wait_recv()
    tc[k] = tx[0] + tx[1] + tx[2] + tx[3]
    got_tc = send(tc.at[k], tc.at[k], tcs.at[0], tcr.at[0], at_core)
    got_bz = [sum_x(0, got_bx[0])]
    got_bx.append(sum_core(1, got_n[1]))
    got_tc.wait_recv()
    w_totals = tc[0][0:1, :] + tc[1][0:1, :]
    places = iota((16, 128), 0)
    own = (places // 2) * 16 + x * 4 + k * 2 + places % 2 == iota((16, 128), 1)
    w_column = jnp.sum(jnp.where(own, w_totals, 0.0), axis=1, keepdims=True)
    got_bz.append(sum_x(1, got_bx[1]))
    got_cz = [sum_z(n, got_bz[n]) for n in range(NC)]

    got = []
    for n in range(NC):
        for copy in got_cz[n]:
            copy.wait_recv()
        got.append(fan_out(hmat2, 1, n))
    got_o = []
    for n in range(NC):
        outr[:, genes(n, z)] = ho[n, z]
        got_o += send_z(lambda s: ho.at[n, s], lambda s: outr.at[:, genes(n, s)], os_.at[n], ors.at[n])

    fan_on(hmat2, 1, 0, got[0])
    fan_in(got[0])

    def h_natural(n):
        cols = slice(n * CH, (n + 1) * CH)
        hn[:, cols] = jnp.dot(
            pick, hmat2[:, :, cols].reshape(128, CH), preferred_element_type=F32
        ).astype(BF)

    def w_part(n, rows):
        acc = None
        for j in range(n * CH // 512, (n + 1) * CH // 512):
            cols = slice(j * 512, (j + 1) * 512)
            modeled = jnp.dot(
                wp[rows, :], hmat2[:, :, cols].reshape(128, 512), preferred_element_type=F32
            )
            counts = cnt[rows, cols].astype(F32)
            quotient = (counts * pltpu.reciprocal(modeled, approx=True)).astype(BF)
            term = lax.dot_general(
                quotient, hn[:, cols], (((1,), (1,)), ((), ())), preferred_element_type=F32
            )
            acc = term if acc is None else acc + term
        return acc

    h_natural(0)
    for i in range(2):
        rows = slice(i * 240, (i + 1) * 240)
        wn[rows, :] = w_part(0, rows)
    fan_on(hmat2, 1, 1, got[1])
    for i in range(2, 4):
        rows = slice(i * 240, (i + 1) * 240)
        wn[rows, :] = w_part(0, rows)
    fan_in(got[1])
    h_natural(1)

    def code_y(part, d, value):
        size = SIZES[part]
        scale = scale_of(value)
        dy[part, d - 1, 0:size, :] = encode(value, scale)
        dy[part, d - 1, size : size + 16, :] = twice(scale)
        whole = pl.ds(0, size + 16)
        return send(
            dy.at[part, d - 1, whole], dyr.at[part, d - 1, whole], dys.at[part, d - 1], dyrs.at[part, d - 1], at_y(d)
        )

    def rows_of(part, owner):
        return pl.ds(pl.multiple_of(owner * ROWS + STARTS[part], 16), SIZES[part])

    def sum_y(part, got):
        size = SIZES[part]
        total = wn[rows_of(part, y), :]
        for d in (1, 3, 2):
            got[d].wait_recv()
            total = total + decode(dyr[part, d - 1, 0:size, :], dyr[part, d - 1, size : size + 16, :])
        scale = scale_of(total)
        dz[part, 0:size, :] = encode(total, scale)
        dz[part, size : size + 16, :] = twice(scale)
        whole = pl.ds(0, size + 16)
        return send(dz.at[part, whole], zr.at[part, whole], dzs.at[part], dzr.at[part], at_zh)

    got_y = [{}, {}]
    got_z = []
    for part in range(2):
        for d in (2, 1, 3, 0):
            rows = rows_of(part, (y + d) % 4)
            value = wn[rows, :] + w_part(1, rows)
            if d:
                got_y[part][d] = code_y(part, d, value)
            else:
                wn[rows, :] = value
            if part == 1 and d == 1:
                got_z.append(sum_y(0, got_y[0]))
    ht[y] = lax.dot_general(
        jnp.ones((8, 2048), BF), hn[...], (((1,), (1,)), ((), ())), preferred_element_type=F32
    )
    got_h = [send(ht.at[y], ht.at[y], hts.at[d - 1], htr.at[d - 1], at_y(d)) for d in (2, 1, 3)]
    got_z.append(sum_y(1, got_y[1]))
    for copy in got_h:
        copy.wait_recv()
    hz[zh] = ht[0] + ht[1] + ht[2] + ht[3]
    got_hz = send(hz.at[zh], hz.at[zh], hzs.at[0], hzr.at[0], at_zh)
    for copy in got_o:
        copy.wait_recv()
    h_out[...] = outr[...]

    got_w = []
    for part in range(2):
        size = SIZES[part]
        got_z[part].wait_recv()
        total = decode(dz[part, 0:size, :], dz[part, size : size + 16, :])
        total = total + decode(zr[part, 0:size, :], zr[part, size : size + 16, :])
        scale = scale_of(total)
        da[part, y, 0:size, :] = encode(total, scale)
        da[part, y, size : size + 16, :] = twice(scale)
        mine = da.at[part, y, pl.ds(0, size + 16)]
        got_w.append({d: send(mine, mine, das.at[part, d - 1], dar.at[part, d - 1], at_y(d)) for d in (2, 1, 3)})
    got_hz.wait_recv()
    h_totals = hz[0] + hz[1]
    for part in range(2):
        size = SIZES[part]
        inverse = spread(1.0 / h_totals, size, 128)
        for d in (0, 1, 3, 2):
            if d:
                got_w[part][d].wait_recv()
            p = (y + 4 - d) % 4
            rows = rows_of(part, p)
            share = decode(da[part, p, 0:size, :], da[part, p, size : size + 16, :])
            w_out[rows, :] = wf[rows, :] * (share * inverse)
    for copy in sent:
        copy.wait_send()


def per_device(counts, w_factor, h_factor):
    vmem = pltpu.VMEM
    dma = pltpu.SemaphoreType.DMA
    far = pl.BlockSpec(memory_space=pl.ANY)
    local = pl.BlockSpec(memory_space=pltpu.VMEM)
    return pl.pallas_call(
        kernel,
        out_shape=(
            jax.ShapeDtypeStruct((960, 128), F32),
            jax.ShapeDtypeStruct((2, 2048), F32),
        ),
        in_specs=[far, far, far],
        out_specs=(local, local),
        scratch_shapes=[
            vmem((960, 2048), BF), vmem((960, 128), F32), vmem((2, 2048), F32), vmem((960, 128), BF), vmem((128, 960), BF),
            vmem((960, CH), BF),
            vmem((2, 2048), BF), vmem((8, 2, 2048), BF), vmem((16, 2048), F32), vmem((8, 16, 2048), BF),
            vmem((8, 8, 128), F32), vmem((8, 8, 128), F32), vmem((NC, 16, ZG), F32),
            vmem((4, 8, 128), F32), vmem((2, 8, 128), F32),
            vmem((NC, 2, 64, CH), F32), vmem((NC, 64, CH), F32), vmem((NC, 4, 16, CH), F32),
            vmem((NC, 4, 16, CH + 128), BF), vmem((NC, 3, 16, CH + 128), BF),
            vmem((NC, 8, 16, ZG), F32), vmem((NC, 8, 16, ZG + 128), BF), vmem((NC, 8, 16, ZG + 128), BF),
            vmem((NC, 16, ZG), BF), vmem((NC, 8, 2, ZG), F32), vmem((2, 2048), F32),
            vmem((8, 16, 2048), BF), vmem((128, 2048), BF), vmem((4, 8, 128), F32), vmem((2, 8, 128), F32),
            vmem((960, 128), F32), vmem((2, 3, 144, 128), BF), vmem((2, 3, 144, 128), BF),
            vmem((2, 144, 128), BF), vmem((2, 144, 128), BF), vmem((2, 4, 144, 128), BF),
            dma((3,)), dma((8,)), dma((8,)), dma((8,)), dma((8,)), dma((3,)), dma((3,)), dma((1,)), dma((1,)),
            dma((2, NC, 3)), dma((2, NC, 3)), dma((2, NC, 4)), dma((2, NC, 4)), dma((NC,)), dma((NC,)),
            dma((NC, 3)), dma((NC, 3)), dma((NC, 8)), dma((NC, 8)), dma((NC, 8)), dma((NC, 8)),
            dma((NC, 8)), dma((NC, 8)), dma((3,)), dma((3,)), dma((1,)), dma((1,)),
            dma((2, 3)), dma((2, 3)), dma((2,)), dma((2,)), dma((2, 3)), dma((2, 3)),
        ],
        compiler_params=pltpu.CompilerParams(
            collective_id=0, has_side_effects=True, vmem_limit_bytes=60 * 1024 * 1024
        ),
        name="nmf_update",
    )(counts, w_factor, h_factor)


def solution(mesh):
    in_specs = (P("cell", "gene"), P("cell", None), P("cell", "gene"))
    out_specs = (P("cell", None), P("cell", "gene"))
    return jax.shard_map(
        per_device, mesh=mesh, in_specs=in_specs, out_specs=out_specs, check_vma=False
    )
```

```python
import jax
import jax.numpy as jnp
from jax import lax
from jax.experimental import pallas as pl
from jax.experimental.pallas import tpu as pltpu
from jax.sharding import PartitionSpec as P

MESH = pl.DeviceIdType.MESH
BF = jnp.bfloat16
F32 = jnp.float32
NC = 2
CH = 2048 // NC
ZG = CH // 8
HALF = CH // 2
ROWS = 240
STARTS, SIZES = (0, 128), (128, 112)
NEAR = (1, 2, 3, 4, 5, 6, 7)
FAR = (7, 6, 5, 4, 3, 2, 1)


def iota(shape, dim):
    return lax.broadcasted_iota(jnp.int32, shape, dim)


def natural(i):
    return ((i % 16) // 2) * 16 + ((i // 16) % 4) * 4 + (i // 64) * 2 + i % 2


def spread(tile, rows, columns):
    wide = jnp.concatenate([tile] * (columns // 128), axis=1) if columns > 128 else tile
    return jnp.concatenate([wide] * (rows // 8), axis=0) if rows > 8 else wide


def scale_of(value):
    rows, columns = value.shape
    top = jnp.full((8, 128), 1e-30, F32)
    for r in range(0, rows, 8):
        for c in range(0, columns, 128):
            top = jnp.maximum(top, value[r : r + 8, c : c + 128])
    return top.astype(BF)


def encode(value, scale):
    rows, columns = value.shape
    share = value * spread(32768.0 / scale.astype(F32), rows, columns)
    square = share * share
    fourth = square * square
    return (fourth * fourth).astype(BF)


def decode(code, scale16):
    rows, columns = code.shape
    unit = scale16[0:8, :].astype(F32) * (1.0 / 32768.0)
    root = jnp.sqrt(jnp.sqrt(jnp.sqrt(code.astype(F32))))
    return root * spread(unit, rows, columns)


def twice(scale):
    wide = scale.astype(F32)
    return jnp.concatenate([wide, wide], axis=0).astype(BF)


def kernel(
    cnt_hbm, w_hbm, h_hbm, w_out, h_out,
    cnt, wf, h_in, wp, wt, quo,
    hown, ha, hx32, hmat, fm, fr, h16, tx, tc,
    num, numr, bs, bx, bxr, tz, bz, bzr, hu, ho, outr, hmat2, hn, ht, hz,
    wn, dy, dyr, dz, zr, da, wv,
    ls, as_, ar, fs, frs, txs, txr, tcs, tcr,
    xs, xr, cs, cr, ns, nr, bxs, bxrs, bzs, bzrs, cz, czr, os_, ors, hts, htr, hzs, hzr,
    dys, dyrs, dzs, dzr, das, dar, gs,
):
    c = lax.axis_index("cell")
    g = lax.axis_index("gene")
    z, x, k = c // 8, (c // 2) % 4, c % 2
    y, zh = g // 2, g % 2
    slot = k * 4 + x

    half = z // 4

    def z_of(d):
        return half * 4 + (z + d) % 4 if d < 4 else half * (7 - d) + (1 - half) * d

    def at_z(d):
        return (z_of(d) * 8 + x * 2 + k, g)

    def at_x(d):
        return (z * 8 + ((x + d) % 4) * 2 + k, g)

    def at_y(d):
        return (c, ((y + d) % 4) * 2 + zh)

    def genes(n, owner):
        return pl.ds(pl.multiple_of(n * CH + owner * ZG, ZG), ZG)

    at_core = (z * 8 + x * 2 + (1 - k), g)
    at_zh = (c, y * 2 + (1 - zh))
    sent = []

    def remote(src, dst, ssem, rsem, device):
        return pltpu.make_async_remote_copy(
            src_ref=src, dst_ref=dst, send_sem=ssem, recv_sem=rsem, device_id=device, device_id_type=MESH
        )

    def due(copy):
        return copy

    def send(src, dst, ssem, rsem, device):
        copy = remote(src, dst, ssem, rsem, device)
        copy.start()
        sent.append(copy)
        return due(copy)

    def send_z(src, dst, ssem, rsem):
        for d in FAR:
            copy = remote(src(z_of(d)), dst(z), ssem.at[d], rsem.at[z], at_z(d))
            copy.start()
            sent.append(copy)
        return [
            due(remote(src(z_of(d)), dst(z_of(d)), ssem.at[d], rsem.at[z_of(d)], at_z(d))) for d in NEAR
        ]

    barrier = pltpu.get_barrier_semaphore()
    friends = [at_z(d) for d in FAR] + [at_x(d) for d in range(1, 4)] + [at_core]
    friends += [at_y(d) for d in range(1, 4)] + [at_zh]
    for friend in friends:
        pl.semaphore_signal(barrier, inc=1, device_id=friend, device_id_type=MESH)

    load_h = pltpu.make_async_copy(h_hbm, h_in, ls.at[2])
    load_w = pltpu.make_async_copy(w_hbm, wf, ls.at[1])
    load_cnt = pltpu.make_async_copy(cnt_hbm, cnt, ls.at[0])
    load_h.start()
    load_w.start()
    load_cnt.start()
    load_h.wait()
    hown[...] = h_in[...].astype(BF)
    pl.semaphore_wait(barrier, len(friends))

    got_a = send_z(lambda s: hown, lambda s: ha.at[s], as_, ar)
    ha[z] = hown[...]

    load_w.wait()
    w_all = wf[...]
    w_sum = jnp.sum(w_all, axis=0, keepdims=True)
    h_own = h_in[...]
    for zz in range(8):
        for n in range(NC):
            base = n * CH + zz * ZG
            fm[zz, 2 * n : 2 * n + 2, :] = h_own[:, base : base + ZG]
        fm[zz, 4:5, :] = w_sum
    got_f = send_z(lambda s: fm.at[s], lambda s: fr.at[s], fs, frs)
    fr[z] = fm[z]
    w_copy = w_all.astype(BF)
    pick = (iota((128, 128), 0) == natural(iota((128, 128), 1))).astype(F32).astype(BF)
    pick_t = (natural(iota((128, 128), 0)) == iota((128, 128), 1)).astype(F32).astype(BF)
    wp[...] = jnp.dot(w_copy, pick, preferred_element_type=F32).astype(BF)
    wt[...] = lax.dot_general(
        pick_t, w_copy, (((1,), (1,)), ((), ())), preferred_element_type=F32
    ).astype(BF)

    for far, copies in ((0, got_a[0:3]), (1, got_a[3:7])):
        for copy in copies:
            copy.wait_recv()
        at = half * (1 - far) + (1 - half) * far
        for j in range(4):
            hx32[at, 2 * j : 2 * j + 2, :] = ha[at * 4 + j].astype(F32)
    hmat[slot] = hx32[...].reshape(16, 2048).astype(BF)

    def fan_out(buf, phase, n, cols):
        mine = buf.at[slot, :, cols]
        got_x = {d: send(mine, mine, xs.at[phase, n, d - 1], xr.at[phase, n, d - 1], at_x(d)) for d in (2, 1, 3)}
        got_c = [send(mine, mine, cs.at[phase, n, 0], cr.at[phase, n, 0], at_core)]
        return got_x, got_c

    def fan_on(buf, phase, n, cols, got):
        for d in (1, 3, 2):
            got[0][d].wait_recv()
            piece = buf.at[k * 4 + (x + 4 - d) % 4, :, cols]
            got[1].append(send(piece, piece, cs.at[phase, n, d], cr.at[phase, n, d], at_core))

    def fan_in(got):
        for copy in got[1]:
            copy.wait_recv()

    def quotients(n, first, last):
        cols = slice(n * CH, (n + 1) * CH)
        h_chunk = hmat[:, :, cols].reshape(128, CH)
        for i in range(first, last):
            rows = slice(i * 120, (i + 1) * 120)
            modeled = jnp.dot(wp[rows, :], h_chunk, preferred_element_type=F32)
            counts = cnt[rows, cols].astype(F32)
            quo[rows, :] = (counts * pltpu.reciprocal(modeled, approx=True)).astype(BF)

    def numerator(n):
        part = jnp.dot(wt[...], quo[...], preferred_element_type=F32)
        num[n, 0] = part[0:64, :]
        num[n, 1] = part[64:128, :]
        return send(num.at[n, 1 - k], numr.at[n], ns.at[n], nr.at[n], at_core)

    def sum_core(n, got):
        got.wait_recv()
        both = num[n, k] + numr[n]
        bs[n] = both.reshape(4, 16, CH)
        scale = scale_of(both)
        code = encode(both, scale)
        scale2 = twice(scale)
        for s in range(4):
            bx[n, s, :, 0:CH] = code[16 * s : 16 * s + 16, :]
            bx[n, s, :, CH : CH + 128] = scale2
        return {
            d: send(bx.at[n, (x + d) % 4], bxr.at[n, d - 1], bxs.at[n, d - 1], bxrs.at[n, d - 1], at_x(d))
            for d in (2, 1, 3)
        }

    def sum_x(n, got):
        total = bs[n, x]
        for d in (1, 3, 2):
            got[d].wait_recv()
            total = total + decode(bxr[n, d - 1, :, 0:CH], bxr[n, d - 1, :, CH : CH + 128])
        scale = scale_of(total)
        code = encode(total, scale)
        scale2 = twice(scale)
        for s in range(8):
            tz[n, s] = total[:, s * ZG : (s + 1) * ZG]
            bz[n, s, :, 0:ZG] = code[:, s * ZG : (s + 1) * ZG]
            bz[n, s, :, ZG : ZG + 128] = scale2
        return send_z(lambda s: bz.at[n, s], lambda s: bzr.at[n, s], bzs.at[n], bzrs.at[n])

    def sum_z(n, got):
        total = tz[n, z]
        for d in NEAR:
            s = z_of(d)
            got[d - 1].wait_recv()
            total = total + decode(bzr[n, s, :, 0:ZG], bzr[n, s, :, ZG : ZG + 128])
        updated = h16[n] * total / w_column
        hu[n] = updated.astype(BF)
        hmat2[slot, :, genes(n, z)] = hu[n]
        copies = send_z(lambda s: hu.at[n], lambda s: hmat2.at[slot, :, genes(n, s)], cz.at[n], czr.at[n])
        for zz in range(8):
            ho[n, zz] = updated[2 * zz : 2 * zz + 2, :]
        return copies

    got = [fan_out(hmat, 0, n, pl.ds(n * CH, CH)) for n in range(NC)]

    for copy in got_f:
        copy.wait_recv()
    tot = jnp.zeros((1, 128), F32)
    for zz in range(8):
        tot = tot + fr[zz, 4:5, :]
        for n in range(NC):
            h16[n, 2 * zz : 2 * zz + 2, :] = fr[zz, 2 * n : 2 * n + 2, :]
    tx[x] = jnp.broadcast_to(tot, (8, 128))
    got_t = [send(tx.at[x], tx.at[x], txs.at[d - 1], txr.at[d - 1], at_x(d)) for d in (2, 1, 3)]
    load_cnt.wait()

    fan_on(hmat, 0, 0, pl.ds(0, CH), got[0])
    fan_in(got[0])
    quotients(0, 0, 4)
    fan_on(hmat, 0, 1, pl.ds(CH, CH), got[1])
    quotients(0, 4, 8)
    got_n = [numerator(0)]
    fan_in(got[1])
    quotients(1, 0, 4)
    got_bx = [sum_core(0, got_n[0])]
    quotients(1, 4, 8)
    got_n.append(numerator(1))
    for copy in got_t:
        copy.wait_recv()
    tc[k] = tx[0] + tx[1] + tx[2] + tx[3]
    got_tc = send(tc.at[k], tc.at[k], tcs.at[0], tcr.at[0], at_core)
    got_bz = [sum_x(0, got_bx[0])]
    got_bx.append(sum_core(1, got_n[1]))
    got_tc.wait_recv()
    w_totals = tc[0][0:1, :] + tc[1][0:1, :]
    places = iota((16, 128), 0)
    own = (places // 2) * 16 + x * 4 + k * 2 + places % 2 == iota((16, 128), 1)
    w_column = jnp.sum(jnp.where(own, w_totals, 0.0), axis=1, keepdims=True)
    got_bz.append(sum_x(1, got_bx[1]))
    got_cz = [sum_z(n, got_bz[n]) for n in range(NC)]

    def columns(piece):
        at = half if piece < 2 else 1 - half
        return pl.ds(pl.multiple_of((piece % 2) * CH + at * HALF, HALF), HALF)

    got = []

    def z_then_out(piece):
        for copy in got_cz[piece % 2][0:3] if piece < 2 else got_cz[piece % 2][3:7]:
            copy.wait_recv()
        got.append(fan_out(hmat2, 1, piece, columns(piece)))

    def pass_on(piece):
        fan_on(hmat2, 1, piece, columns(piece), got[piece])

    z_then_out(0)
    z_then_out(1)
    z_then_out(2)
    pass_on(0)
    z_then_out(3)
    pass_on(1)
    got_o = []
    for n in range(NC):
        outr[:, genes(n, z)] = ho[n, z]
        got_o += send_z(lambda s: ho.at[n, s], lambda s: outr.at[:, genes(n, s)], os_.at[n], ors.at[n])
    fan_in(got[0])
    fan_in(got[1])

    def h_natural(piece):
        cols = columns(piece)
        hn[:, cols] = jnp.dot(
            pick, hmat2[:, :, cols].reshape(128, HALF), preferred_element_type=F32
        ).astype(BF)

    def w_part(far, rows):
        acc = None
        for piece in (2 * far, 2 * far + 1):
            cols = columns(piece)
            modeled = jnp.dot(
                wp[rows, :], hmat2[:, :, cols].reshape(128, HALF), preferred_element_type=F32
            )
            counts = cnt[rows, cols].astype(F32)
            quotient = (counts * pltpu.reciprocal(modeled, approx=True)).astype(BF)
            term = lax.dot_general(
                quotient, hn[:, cols], (((1,), (1,)), ((), ())), preferred_element_type=F32
            )
            acc = term if acc is None else acc + term
        return acc

    h_natural(0)
    h_natural(1)
    for i in range(4):
        rows = slice(i * 240, (i + 1) * 240)
        wn[rows, :] = w_part(0, rows)
        if i == 1:
            pass_on(2)
    pass_on(3)
    fan_in(got[2])
    fan_in(got[3])
    h_natural(2)
    h_natural(3)

    def code_y(part, d, value):
        size = SIZES[part]
        scale = scale_of(value)
        dy[part, d - 1, 0:size, :] = encode(value, scale)
        dy[part, d - 1, size : size + 16, :] = twice(scale)
        whole = pl.ds(0, size + 16)
        return send(
            dy.at[part, d - 1, whole], dyr.at[part, d - 1, whole], dys.at[part, d - 1], dyrs.at[part, d - 1], at_y(d)
        )

    def rows_of(part, owner):
        return pl.ds(pl.multiple_of(owner * ROWS + STARTS[part], 16), SIZES[part])

    def sum_y(part, got):
        size = SIZES[part]
        total = wn[rows_of(part, y), :]
        for d in (1, 3, 2):
            got[d].wait_recv()
            total = total + decode(dyr[part, d - 1, 0:size, :], dyr[part, d - 1, size : size + 16, :])
        scale = scale_of(total)
        dz[part, 0:size, :] = encode(total, scale)
        dz[part, size : size + 16, :] = twice(scale)
        whole = pl.ds(0, size + 16)
        return send(dz.at[part, whole], zr.at[part, whole], dzs.at[part], dzr.at[part], at_zh)

    got_y = [{}, {}]
    got_z = []
    for part in range(2):
        for d in (2, 1, 3, 0):
            rows = rows_of(part, (y + d) % 4)
            value = wn[rows, :] + w_part(1, rows)
            if d:
                got_y[part][d] = code_y(part, d, value)
            else:
                wn[rows, :] = value
            if part == 1 and d == 1:
                got_z.append(sum_y(0, got_y[0]))
    ht[y] = lax.dot_general(
        jnp.ones((8, 2048), BF), hn[...], (((1,), (1,)), ((), ())), preferred_element_type=F32
    )
    got_h = [send(ht.at[y], ht.at[y], hts.at[d - 1], htr.at[d - 1], at_y(d)) for d in (2, 1, 3)]
    got_z.append(sum_y(1, got_y[1]))
    for copy in got_h:
        copy.wait_recv()
    hz[zh] = ht[0] + ht[1] + ht[2] + ht[3]
    got_hz = send(hz.at[zh], hz.at[zh], hzs.at[0], hzr.at[0], at_zh)
    for copy in got_o:
        copy.wait_recv()
    give_h = pltpu.make_async_copy(outr, h_out, ls.at[2])
    give_h.start()

    got_w = []
    for part in range(2):
        size = SIZES[part]
        got_z[part].wait_recv()
        total = decode(dz[part, 0:size, :], dz[part, size : size + 16, :])
        total = total + decode(zr[part, 0:size, :], zr[part, size : size + 16, :])
        scale = scale_of(total)
        da[part, y, 0:size, :] = encode(total, scale)
        da[part, y, size : size + 16, :] = twice(scale)
        mine = da.at[part, y, pl.ds(0, size + 16)]
        got_w.append({d: send(mine, mine, das.at[part, d - 1], dar.at[part, d - 1], at_y(d)) for d in (2, 1, 3)})
    got_hz.wait_recv()
    h_totals = hz[0] + hz[1]
    gives = [give_h]
    for part in range(2):
        size = SIZES[part]
        inverse = spread(1.0 / h_totals, size, 128)
        for d in (0, 1, 3, 2):
            if d:
                got_w[part][d].wait_recv()
            p = (y + 4 - d) % 4
            rows = rows_of(part, p)
            share = decode(da[part, p, 0:size, :], da[part, p, size : size + 16, :])
            wv[rows, :] = wf[rows, :] * (share * inverse)
            given = pltpu.make_async_copy(wv.at[rows, :], w_out.at[rows, :], gs.at[part, d])
            given.start()
            gives.append(given)
    for copy in sent:
        copy.wait_send()
    for given in gives:
        given.wait()


def hand_on(w_in, h_in, w_out, h_out, sems):
    copies = [pltpu.make_async_copy(h_in, h_out, sems.at[4])]
    for i in range(4):
        rows = pl.ds(i * ROWS, ROWS)
        copies.append(pltpu.make_async_copy(w_in.at[rows, :], w_out.at[rows, :], sems.at[i]))
    for copy in copies:
        copy.start()
    for copy in copies:
        copy.wait()


def per_device(counts, w_factor, h_factor):
    vmem = pltpu.VMEM
    dma = pltpu.SemaphoreType.DMA
    far = pl.BlockSpec(memory_space=pl.ANY)
    shapes = (jax.ShapeDtypeStruct((960, 128), F32), jax.ShapeDtypeStruct((2, 2048), F32))
    results = pl.pallas_call(
        kernel,
        out_shape=shapes,
        in_specs=[far, far, far],
        out_specs=(far, far),
        scratch_shapes=[
            vmem((960, 2048), BF), vmem((960, 128), F32), vmem((2, 2048), F32), vmem((960, 128), BF), vmem((128, 960), BF),
            vmem((960, CH), BF),
            vmem((2, 2048), BF), vmem((8, 2, 2048), BF), vmem((2, 8, 2048), F32), vmem((8, 16, 2048), BF),
            vmem((8, 8, 128), F32), vmem((8, 8, 128), F32), vmem((NC, 16, ZG), F32),
            vmem((4, 8, 128), F32), vmem((2, 8, 128), F32),
            vmem((NC, 2, 64, CH), F32), vmem((NC, 64, CH), F32), vmem((NC, 4, 16, CH), F32),
            vmem((NC, 4, 16, CH + 128), BF), vmem((NC, 3, 16, CH + 128), BF),
            vmem((NC, 8, 16, ZG), F32), vmem((NC, 8, 16, ZG + 128), BF), vmem((NC, 8, 16, ZG + 128), BF),
            vmem((NC, 16, ZG), BF), vmem((NC, 8, 2, ZG), F32), vmem((2, 2048), F32),
            vmem((8, 16, 2048), BF), vmem((128, 2048), BF), vmem((4, 8, 128), F32), vmem((2, 8, 128), F32),
            vmem((960, 128), F32), vmem((2, 3, 144, 128), BF), vmem((2, 3, 144, 128), BF),
            vmem((2, 144, 128), BF), vmem((2, 144, 128), BF), vmem((2, 4, 144, 128), BF), vmem((960, 128), F32),
            dma((3,)), dma((8,)), dma((8,)), dma((8,)), dma((8,)), dma((3,)), dma((3,)), dma((1,)), dma((1,)),
            dma((2, 4, 3)), dma((2, 4, 3)), dma((2, 4, 4)), dma((2, 4, 4)), dma((NC,)), dma((NC,)),
            dma((NC, 3)), dma((NC, 3)), dma((NC, 8)), dma((NC, 8)), dma((NC, 8)), dma((NC, 8)),
            dma((NC, 8)), dma((NC, 8)), dma((3,)), dma((3,)), dma((1,)), dma((1,)),
            dma((2, 3)), dma((2, 3)), dma((2,)), dma((2,)), dma((2, 3)), dma((2, 3)), dma((2, 4)),
        ],
        compiler_params=pltpu.CompilerParams(
            collective_id=0, has_side_effects=True, vmem_limit_bytes=60 * 1024 * 1024
        ),
        name="nmf_update",
    )(counts, w_factor, h_factor)
    return pl.pallas_call(
        hand_on,
        out_shape=shapes,
        in_specs=[far, far],
        out_specs=(far, far),
        scratch_shapes=[dma((5,))],
        name="hand_on",
    )(*results)


def solution(mesh):
    in_specs = (P("cell", "gene"), P("cell", None), P("cell", "gene"))
    out_specs = (P("cell", None), P("cell", "gene"))
    return jax.shard_map(
        per_device, mesh=mesh, in_specs=in_specs, out_specs=out_specs, check_vma=False
    )
```

```python
import jax
import jax.numpy as jnp
from jax import lax
from jax.experimental import pallas as pl
from jax.experimental.pallas import tpu as pltpu
from jax.sharding import PartitionSpec as P

MESH = pl.DeviceIdType.MESH
BF = jnp.bfloat16
F32 = jnp.float32
NC = 2
CH = 2048 // NC
ZG = CH // 8
HALF = CH // 2
ROWS = 240
STARTS, SIZES = (0, 128), (128, 112)
NEAR = (1, 2, 3, 4, 5, 6, 7)
FAR = (7, 6, 5, 4, 3, 2, 1)


def iota(shape, dim):
    return lax.broadcasted_iota(jnp.int32, shape, dim)


def natural(i):
    return ((i % 16) // 2) * 16 + ((i // 16) % 4) * 4 + (i // 64) * 2 + i % 2


def spread(tile, rows, columns):
    wide = jnp.concatenate([tile] * (columns // 128), axis=1) if columns > 128 else tile
    return jnp.concatenate([wide] * (rows // 8), axis=0) if rows > 8 else wide


def scale_of(value):
    rows, columns = value.shape
    top = jnp.full((8, 128), 1e-30, F32)
    for r in range(0, rows, 8):
        for c in range(0, columns, 128):
            top = jnp.maximum(top, value[r : r + 8, c : c + 128])
    return top.astype(BF)


def encode(value, scale):
    rows, columns = value.shape
    share = value * spread(32768.0 / scale.astype(F32), rows, columns)
    square = share * share
    fourth = square * square
    return (fourth * fourth).astype(BF)


def decode(code, scale16):
    rows, columns = code.shape
    unit = scale16[0:8, :].astype(F32) * (1.0 / 32768.0)
    root = jnp.sqrt(jnp.sqrt(jnp.sqrt(code.astype(F32))))
    return root * spread(unit, rows, columns)


def twice(scale):
    wide = scale.astype(F32)
    return jnp.concatenate([wide, wide], axis=0).astype(BF)


def kernel(
    cnt_hbm, w_hbm, h_hbm, w_out, h_out,
    cnt, wf, h_in, wp, wt, quo,
    hown, ha, hx32, hmat, fm, fr, h16, tx, tc,
    num, numr, bs, bx, bxr, tz, bz, bzr, hu, ho, outr, hmat2, hn, ht, hz,
    wn, dy, dyr, dz, zr, da, wv,
    ls, as_, ar, fs, frs, txs, txr, tcs, tcr,
    xs, xr, cs, cr, ns, nr, bxs, bxrs, bzs, bzrs, cz, czr, os_, ors, hts, htr, hzs, hzr,
    dys, dyrs, dzs, dzr, das, dar, gs,
):
    c = lax.axis_index("cell")
    g = lax.axis_index("gene")
    z, x, k = c // 8, (c // 2) % 4, c % 2
    y, zh = g // 2, g % 2
    slot = k * 4 + x

    half = z // 4

    def z_of(d):
        return half * 4 + (z + d) % 4 if d < 4 else half * (7 - d) + (1 - half) * d

    def at_z(d):
        return (z_of(d) * 8 + x * 2 + k, g)

    def at_x(d):
        return (z * 8 + ((x + d) % 4) * 2 + k, g)

    def at_y(d):
        return (c, ((y + d) % 4) * 2 + zh)

    def genes(n, owner):
        return pl.ds(pl.multiple_of(n * CH + owner * ZG, ZG), ZG)

    at_core = (z * 8 + x * 2 + (1 - k), g)
    at_zh = (c, y * 2 + (1 - zh))
    sent = []

    def remote(src, dst, ssem, rsem, device):
        return pltpu.make_async_remote_copy(
            src_ref=src, dst_ref=dst, send_sem=ssem, recv_sem=rsem, device_id=device, device_id_type=MESH
        )

    def due(copy):
        return copy

    def send(src, dst, ssem, rsem, device):
        copy = remote(src, dst, ssem, rsem, device)
        copy.start()
        sent.append(copy)
        return due(copy)

    def send_z(src, dst, ssem, rsem):
        for d in FAR:
            copy = remote(src(z_of(d)), dst(z), ssem.at[d], rsem.at[z], at_z(d))
            copy.start()
            sent.append(copy)
        return [
            due(remote(src(z_of(d)), dst(z_of(d)), ssem.at[d], rsem.at[z_of(d)], at_z(d))) for d in NEAR
        ]

    barrier = pltpu.get_barrier_semaphore()
    friends = [at_z(d) for d in FAR] + [at_x(d) for d in range(1, 4)] + [at_core]
    friends += [at_y(d) for d in range(1, 4)] + [at_zh]
    for friend in friends:
        pl.semaphore_signal(barrier, inc=1, device_id=friend, device_id_type=MESH)

    load_h = pltpu.make_async_copy(h_hbm, h_in, ls.at[2])
    load_w = pltpu.make_async_copy(w_hbm, wf, ls.at[1])
    load_cnt = pltpu.make_async_copy(cnt_hbm, cnt, ls.at[0])
    load_h.start()
    load_w.start()
    load_cnt.start()
    load_h.wait()
    hown[...] = h_in[...].astype(BF)
    pl.semaphore_wait(barrier, len(friends))

    got_a = send_z(lambda s: hown, lambda s: ha.at[s], as_, ar)
    ha[z] = hown[...]

    load_w.wait()
    w_all = wf[...]
    w_sum = jnp.sum(w_all, axis=0, keepdims=True)
    h_own = h_in[...]
    for zz in range(8):
        for n in range(NC):
            base = n * CH + zz * ZG
            fm[zz, 2 * n : 2 * n + 2, :] = h_own[:, base : base + ZG]
        fm[zz, 4:5, :] = w_sum
    got_f = send_z(lambda s: fm.at[s], lambda s: fr.at[s], fs, frs)
    fr[z] = fm[z]
    w_copy = w_all.astype(BF)
    pick = (iota((128, 128), 0) == natural(iota((128, 128), 1))).astype(F32).astype(BF)
    pick_t = (natural(iota((128, 128), 0)) == iota((128, 128), 1)).astype(F32).astype(BF)
    wp[...] = jnp.dot(w_copy, pick, preferred_element_type=F32).astype(BF)
    wt[...] = lax.dot_general(
        pick_t, w_copy, (((1,), (1,)), ((), ())), preferred_element_type=F32
    ).astype(BF)

    for far, copies in ((0, got_a[0:3]), (1, got_a[3:7])):
        for copy in copies:
            copy.wait_recv()
        at = half * (1 - far) + (1 - half) * far
        for j in range(4):
            hx32[at, 2 * j : 2 * j + 2, :] = ha[at * 4 + j].astype(F32)
    hmat[slot] = hx32[...].reshape(16, 2048).astype(BF)

    def fan_out(buf, phase, n, cols):
        mine = buf.at[slot, :, cols]
        got_x = {d: send(mine, mine, xs.at[phase, n, d - 1], xr.at[phase, n, d - 1], at_x(d)) for d in (2, 1, 3)}
        got_c = [send(mine, mine, cs.at[phase, n, 0], cr.at[phase, n, 0], at_core)]
        return got_x, got_c

    def fan_on(buf, phase, n, cols, got):
        for d in (1, 3, 2):
            got[0][d].wait_recv()
            piece = buf.at[k * 4 + (x + 4 - d) % 4, :, cols]
            got[1].append(send(piece, piece, cs.at[phase, n, d], cr.at[phase, n, d], at_core))

    def fan_in(got):
        for copy in got[1]:
            copy.wait_recv()

    def quotients(n, first, last):
        cols = slice(n * CH, (n + 1) * CH)
        h_chunk = hmat[:, :, cols].reshape(128, CH)
        for i in range(first, last):
            rows = slice(i * 120, (i + 1) * 120)
            modeled = jnp.dot(wp[rows, :], h_chunk, preferred_element_type=F32)
            counts = cnt[rows, cols].astype(F32)
            quo[rows, :] = (counts * pltpu.reciprocal(modeled, approx=True)).astype(BF)

    def numerator(n):
        part = jnp.dot(wt[...], quo[...], preferred_element_type=F32)
        num[n, 0] = part[0:64, :]
        num[n, 1] = part[64:128, :]
        return send(num.at[n, 1 - k], numr.at[n], ns.at[n], nr.at[n], at_core)

    def sum_core(n, got):
        got.wait_recv()
        both = num[n, k] + numr[n]
        bs[n] = both.reshape(4, 16, CH)
        scale = scale_of(both)
        code = encode(both, scale)
        scale2 = twice(scale)
        for s in range(4):
            bx[n, s, :, 0:CH] = code[16 * s : 16 * s + 16, :]
            bx[n, s, :, CH : CH + 128] = scale2
        return {
            d: send(bx.at[n, (x + d) % 4], bxr.at[n, d - 1], bxs.at[n, d - 1], bxrs.at[n, d - 1], at_x(d))
            for d in (2, 1, 3)
        }

    def sum_x(n, got):
        total = bs[n, x]
        for d in (1, 3, 2):
            got[d].wait_recv()
            total = total + decode(bxr[n, d - 1, :, 0:CH], bxr[n, d - 1, :, CH : CH + 128])
        scale = scale_of(total)
        code = encode(total, scale)
        scale2 = twice(scale)
        for s in range(8):
            tz[n, s] = total[:, s * ZG : (s + 1) * ZG]
            bz[n, s, :, 0:ZG] = code[:, s * ZG : (s + 1) * ZG]
            bz[n, s, :, ZG : ZG + 128] = scale2
        return send_z(lambda s: bz.at[n, s], lambda s: bzr.at[n, s], bzs.at[n], bzrs.at[n])

    def sum_z(n, got):
        total = tz[n, z]
        for d in NEAR:
            s = z_of(d)
            got[d - 1].wait_recv()
            total = total + decode(bzr[n, s, :, 0:ZG], bzr[n, s, :, ZG : ZG + 128])
        updated = h16[n] * total / w_column
        hu[n] = updated.astype(BF)
        hmat2[slot, :, genes(n, z)] = hu[n]
        copies = send_z(lambda s: hu.at[n], lambda s: hmat2.at[slot, :, genes(n, s)], cz.at[n], czr.at[n])
        for zz in range(8):
            ho[n, zz] = updated[2 * zz : 2 * zz + 2, :]
        return copies

    got = [fan_out(hmat, 0, n, pl.ds(n * CH, CH)) for n in range(NC)]

    for copy in got_f:
        copy.wait_recv()
    tot = jnp.zeros((1, 128), F32)
    for zz in range(8):
        tot = tot + fr[zz, 4:5, :]
        for n in range(NC):
            h16[n, 2 * zz : 2 * zz + 2, :] = fr[zz, 2 * n : 2 * n + 2, :]
    tx[x] = jnp.broadcast_to(tot, (8, 128))
    got_t = [send(tx.at[x], tx.at[x], txs.at[d - 1], txr.at[d - 1], at_x(d)) for d in (2, 1, 3)]
    load_cnt.wait()

    fan_on(hmat, 0, 0, pl.ds(0, CH), got[0])
    fan_on(hmat, 0, 1, pl.ds(CH, CH), got[1])
    got_n = []
    for n in range(NC):
        fan_in(got[n])
        quotients(n, 0, 8)
        got_n.append(numerator(n))
    got_bx = [sum_core(0, got_n[0])]
    for copy in got_t:
        copy.wait_recv()
    tc[k] = tx[0] + tx[1] + tx[2] + tx[3]
    got_tc = send(tc.at[k], tc.at[k], tcs.at[0], tcr.at[0], at_core)
    got_bx.append(sum_core(1, got_n[1]))
    got_tc.wait_recv()
    w_totals = tc[0][0:1, :] + tc[1][0:1, :]
    places = iota((16, 128), 0)
    own = (places // 2) * 16 + x * 4 + k * 2 + places % 2 == iota((16, 128), 1)
    w_column = jnp.sum(jnp.where(own, w_totals, 0.0), axis=1, keepdims=True)
    got_bz = [sum_x(n, got_bx[n]) for n in range(NC)]
    got_cz = [sum_z(n, got_bz[n]) for n in range(NC)]

    def columns(piece):
        at = half if piece < 2 else 1 - half
        return pl.ds(pl.multiple_of((piece % 2) * CH + at * HALF, HALF), HALF)

    got = []

    def z_then_out(piece):
        for copy in got_cz[piece % 2][0:3] if piece < 2 else got_cz[piece % 2][3:7]:
            copy.wait_recv()
        got.append(fan_out(hmat2, 1, piece, columns(piece)))

    def pass_on(piece):
        fan_on(hmat2, 1, piece, columns(piece), got[piece])

    z_then_out(0)
    z_then_out(1)
    z_then_out(2)
    pass_on(0)
    z_then_out(3)
    pass_on(1)
    got_o = []
    for n in range(NC):
        outr[:, genes(n, z)] = ho[n, z]
        got_o += send_z(lambda s: ho.at[n, s], lambda s: outr.at[:, genes(n, s)], os_.at[n], ors.at[n])
    fan_in(got[0])
    fan_in(got[1])

    def h_natural(piece):
        cols = columns(piece)
        hn[:, cols] = jnp.dot(
            pick, hmat2[:, :, cols].reshape(128, HALF), preferred_element_type=F32
        ).astype(BF)

    def w_part(far, rows):
        acc = None
        for piece in (2 * far, 2 * far + 1):
            cols = columns(piece)
            modeled = jnp.dot(
                wp[rows, :], hmat2[:, :, cols].reshape(128, HALF), preferred_element_type=F32
            )
            counts = cnt[rows, cols].astype(F32)
            quotient = (counts * pltpu.reciprocal(modeled, approx=True)).astype(BF)
            term = lax.dot_general(
                quotient, hn[:, cols], (((1,), (1,)), ((), ())), preferred_element_type=F32
            )
            acc = term if acc is None else acc + term
        return acc

    h_natural(0)
    h_natural(1)
    for i in range(4):
        rows = slice(i * 240, (i + 1) * 240)
        wn[rows, :] = w_part(0, rows)
        if i == 1:
            pass_on(2)
    pass_on(3)
    fan_in(got[2])
    fan_in(got[3])
    h_natural(2)
    h_natural(3)

    def code_y(part, d, value):
        size = SIZES[part]
        scale = scale_of(value)
        dy[part, d - 1, 0:size, :] = encode(value, scale)
        dy[part, d - 1, size : size + 16, :] = twice(scale)
        whole = pl.ds(0, size + 16)
        return send(
            dy.at[part, d - 1, whole], dyr.at[part, d - 1, whole], dys.at[part, d - 1], dyrs.at[part, d - 1], at_y(d)
        )

    def rows_of(part, owner):
        return pl.ds(pl.multiple_of(owner * ROWS + STARTS[part], 16), SIZES[part])

    def sum_y(part, got):
        size = SIZES[part]
        total = wn[rows_of(part, y), :]
        for d in (1, 3, 2):
            got[d].wait_recv()
            total = total + decode(dyr[part, d - 1, 0:size, :], dyr[part, d - 1, size : size + 16, :])
        scale = scale_of(total)
        dz[part, 0:size, :] = encode(total, scale)
        dz[part, size : size + 16, :] = twice(scale)
        whole = pl.ds(0, size + 16)
        return send(dz.at[part, whole], zr.at[part, whole], dzs.at[part], dzr.at[part], at_zh)

    got_y = [{}, {}]
    got_z = []
    for part in range(2):
        for d in (2, 1, 3, 0):
            rows = rows_of(part, (y + d) % 4)
            value = wn[rows, :] + w_part(1, rows)
            if d:
                got_y[part][d] = code_y(part, d, value)
            else:
                wn[rows, :] = value
    ht[y] = lax.dot_general(
        jnp.ones((8, 2048), BF), hn[...], (((1,), (1,)), ((), ())), preferred_element_type=F32
    )
    got_h = [send(ht.at[y], ht.at[y], hts.at[d - 1], htr.at[d - 1], at_y(d)) for d in (2, 1, 3)]
    got_z += [sum_y(part, got_y[part]) for part in range(2)]
    for copy in got_h:
        copy.wait_recv()
    hz[zh] = ht[0] + ht[1] + ht[2] + ht[3]
    got_hz = send(hz.at[zh], hz.at[zh], hzs.at[0], hzr.at[0], at_zh)
    for copy in got_o:
        copy.wait_recv()
    give_h = pltpu.make_async_copy(outr, h_out, ls.at[2])
    give_h.start()

    got_w = []
    for part in range(2):
        size = SIZES[part]
        got_z[part].wait_recv()
        total = decode(dz[part, 0:size, :], dz[part, size : size + 16, :])
        total = total + decode(zr[part, 0:size, :], zr[part, size : size + 16, :])
        scale = scale_of(total)
        da[part, y, 0:size, :] = encode(total, scale)
        da[part, y, size : size + 16, :] = twice(scale)
        mine = da.at[part, y, pl.ds(0, size + 16)]
        got_w.append({d: send(mine, mine, das.at[part, d - 1], dar.at[part, d - 1], at_y(d)) for d in (2, 1, 3)})
    got_hz.wait_recv()
    h_totals = hz[0] + hz[1]
    gives = [give_h]
    for part in range(2):
        size = SIZES[part]
        inverse = spread(1.0 / h_totals, size, 128)
        for d in (0, 1, 3, 2):
            if d:
                got_w[part][d].wait_recv()
            p = (y + 4 - d) % 4
            rows = rows_of(part, p)
            share = decode(da[part, p, 0:size, :], da[part, p, size : size + 16, :])
            wv[rows, :] = wf[rows, :] * (share * inverse)
            given = pltpu.make_async_copy(wv.at[rows, :], w_out.at[rows, :], gs.at[part, d])
            given.start()
            gives.append(given)
    for copy in sent:
        copy.wait_send()
    for given in gives:
        given.wait()


def hand_on(w_in, h_in, w_out, h_out, w_mid, h_mid, sems):
    moves = [(h_in, h_mid, h_out)]
    for i in range(4):
        rows = pl.ds(i * ROWS, ROWS)
        moves.append((w_in.at[rows, :], w_mid.at[rows, :], w_out.at[rows, :]))
    arrive = [pltpu.make_async_copy(src, mid, sems.at[0, i]) for i, (src, mid, dst) in enumerate(moves)]
    leave = [pltpu.make_async_copy(mid, dst, sems.at[1, i]) for i, (src, mid, dst) in enumerate(moves)]
    for copy in arrive:
        copy.start()
    for before, after in zip(arrive, leave):
        before.wait()
        after.start()
    for copy in leave:
        copy.wait()


def per_device(counts, w_factor, h_factor):
    vmem = pltpu.VMEM
    dma = pltpu.SemaphoreType.DMA
    far = pl.BlockSpec(memory_space=pl.ANY)
    shapes = (jax.ShapeDtypeStruct((960, 128), F32), jax.ShapeDtypeStruct((2, 2048), F32))
    results = pl.pallas_call(
        kernel,
        out_shape=shapes,
        in_specs=[far, far, far],
        out_specs=(far, far),
        scratch_shapes=[
            vmem((960, 2048), BF), vmem((960, 128), F32), vmem((2, 2048), F32), vmem((960, 128), BF), vmem((128, 960), BF),
            vmem((960, CH), BF),
            vmem((2, 2048), BF), vmem((8, 2, 2048), BF), vmem((2, 8, 2048), F32), vmem((8, 16, 2048), BF),
            vmem((8, 8, 128), F32), vmem((8, 8, 128), F32), vmem((NC, 16, ZG), F32),
            vmem((4, 8, 128), F32), vmem((2, 8, 128), F32),
            vmem((NC, 2, 64, CH), F32), vmem((NC, 64, CH), F32), vmem((NC, 4, 16, CH), F32),
            vmem((NC, 4, 16, CH + 128), BF), vmem((NC, 3, 16, CH + 128), BF),
            vmem((NC, 8, 16, ZG), F32), vmem((NC, 8, 16, ZG + 128), BF), vmem((NC, 8, 16, ZG + 128), BF),
            vmem((NC, 16, ZG), BF), vmem((NC, 8, 2, ZG), F32), vmem((2, 2048), F32),
            vmem((8, 16, 2048), BF), vmem((128, 2048), BF), vmem((4, 8, 128), F32), vmem((2, 8, 128), F32),
            vmem((960, 128), F32), vmem((2, 3, 144, 128), BF), vmem((2, 3, 144, 128), BF),
            vmem((2, 144, 128), BF), vmem((2, 144, 128), BF), vmem((2, 4, 144, 128), BF), vmem((960, 128), F32),
            dma((3,)), dma((8,)), dma((8,)), dma((8,)), dma((8,)), dma((3,)), dma((3,)), dma((1,)), dma((1,)),
            dma((2, 4, 3)), dma((2, 4, 3)), dma((2, 4, 4)), dma((2, 4, 4)), dma((NC,)), dma((NC,)),
            dma((NC, 3)), dma((NC, 3)), dma((NC, 8)), dma((NC, 8)), dma((NC, 8)), dma((NC, 8)),
            dma((NC, 8)), dma((NC, 8)), dma((3,)), dma((3,)), dma((1,)), dma((1,)),
            dma((2, 3)), dma((2, 3)), dma((2,)), dma((2,)), dma((2, 3)), dma((2, 3)), dma((2, 4)),
        ],
        compiler_params=pltpu.CompilerParams(
            collective_id=0, has_side_effects=True, vmem_limit_bytes=56 * 1024 * 1024
        ),
        name="nmf_update",
    )(counts, w_factor, h_factor)
    return pl.pallas_call(
        hand_on,
        out_shape=shapes,
        in_specs=[far, far],
        out_specs=(far, far),
        scratch_shapes=[vmem((960, 128), F32), vmem((2, 2048), F32), dma((2, 5))],
        name="hand_on",
    )(*results)


def solution(mesh):
    in_specs = (P("cell", "gene"), P("cell", None), P("cell", "gene"))
    out_specs = (P("cell", None), P("cell", "gene"))
    return jax.shard_map(
        per_device, mesh=mesh, in_specs=in_specs, out_specs=out_specs, check_vma=False
    )
```

```python
import jax
import jax.numpy as jnp
from jax import lax
from jax.experimental import pallas as pl
from jax.experimental.pallas import tpu as pltpu
from jax.sharding import PartitionSpec as P

MESH = pl.DeviceIdType.MESH
BF = jnp.bfloat16
F32 = jnp.float32
NC = 2
CH = 2048 // NC
ZG = CH // 4
LOW = 2
HALF = CH // 2
ROWS = 240
STARTS, SIZES = (0, 128), (128, 112)
NEAR = (1, 2, 3, 4, 5, 6, 7)
FAR = (7, 6, 5, 4, 3, 2, 1)


def iota(shape, dim):
    return lax.broadcasted_iota(jnp.int32, shape, dim)


def natural(i):
    return ((i % 16) // 2) * 16 + ((i // 16) % 4) * 4 + (i // 64) * 2 + i % 2


def spread(tile, rows, columns):
    wide = jnp.concatenate([tile] * (columns // 128), axis=1) if columns > 128 else tile
    return jnp.concatenate([wide] * (rows // 8), axis=0) if rows > 8 else wide


def scale_of(value):
    rows, columns = value.shape
    top = jnp.full((8, 128), 1e-30, F32)
    for r in range(0, rows, 8):
        for c in range(0, columns, 128):
            top = jnp.maximum(top, value[r : r + 8, c : c + 128])
    return top.astype(BF)


def encode(value, scale):
    rows, columns = value.shape
    share = value * spread(32768.0 / scale.astype(F32), rows, columns)
    square = share * share
    fourth = square * square
    return (fourth * fourth).astype(BF)


def decode(code, scale16):
    rows, columns = code.shape
    unit = scale16[0:8, :].astype(F32) * (1.0 / 32768.0)
    root = jnp.sqrt(jnp.sqrt(jnp.sqrt(code.astype(F32))))
    return root * spread(unit, rows, columns)


def twice(scale):
    wide = scale.astype(F32)
    return jnp.concatenate([wide, wide], axis=0).astype(BF)


def kernel(
    cnt_hbm, w_hbm, h_hbm, w_out, h_out,
    cnt, wf, h_in, wp, wt, quo,
    hown, ha, hx32, hmat, fm, fr, h16, tx, tc,
    num, numr, bs, bx, bxr, tz, bz, bzr, hu, ho, outr, hmat2, hn, ht, hz,
    wn, dy, dyr, dz, zr, da, wv,
    ls, as_, ar, fs, frs, txs, txr, tcs, tcr,
    xs, xr, cs, cr, ns, nr, bxs, bxrs, bzs, bzrs, cz, czr, os_, ors, hts, htr, hzs, hzr,
    dys, dyrs, dzs, dzr, das, dar, gs,
):
    c = lax.axis_index("cell")
    g = lax.axis_index("gene")
    z, x, k = c // 8, (c // 2) % 4, c % 2
    y, zh = g // 2, g % 2
    slot = k * 4 + x

    half = z // 4

    def z_of(d):
        return half * 4 + (z + d) % 4 if d < 4 else half * (7 - d) + (1 - half) * d

    def at_z(d):
        return (z_of(d) * 8 + x * 2 + k, g)

    def at_x(d):
        return (z * 8 + ((x + d) % 4) * 2 + k, g)

    def at_y(d):
        return (c, ((y + d) % 4) * 2 + zh)

    def genes(n, owner):
        return pl.ds(pl.multiple_of(n * CH + owner * ZG, ZG), ZG)

    at_core = (z * 8 + x * 2 + (1 - k), g)
    at_zh = (c, y * 2 + (1 - zh))
    sent = []

    def remote(src, dst, ssem, rsem, device):
        return pltpu.make_async_remote_copy(
            src_ref=src, dst_ref=dst, send_sem=ssem, recv_sem=rsem, device_id=device, device_id_type=MESH
        )

    def due(copy):
        return copy

    def send(src, dst, ssem, rsem, device):
        copy = remote(src, dst, ssem, rsem, device)
        copy.start()
        sent.append(copy)
        return due(copy)

    def send_z(src, dst, ssem, rsem):
        for d in FAR:
            copy = remote(src(z_of(d)), dst(z), ssem.at[d], rsem.at[z], at_z(d))
            copy.start()
            sent.append(copy)
        return [
            due(remote(src(z_of(d)), dst(z_of(d)), ssem.at[d], rsem.at[z_of(d)], at_z(d))) for d in NEAR
        ]

    barrier = pltpu.get_barrier_semaphore()
    friends = [at_z(d) for d in FAR] + [at_x(d) for d in range(1, 4)] + [at_core]
    friends += [at_y(d) for d in range(1, 4)] + [at_zh]
    for friend in friends:
        pl.semaphore_signal(barrier, inc=1, device_id=friend, device_id_type=MESH)

    is_owner = jnp.logical_and(z >= LOW, z < LOW + 4)
    mine = jnp.clip(z - LOW, 0, 3)
    sent_if = []

    def to_owners(src, dst, ssem, rsem):
        for j in range(4):
            device = ((LOW + j) * 8 + x * 2 + k, g)
            copy = remote(src(j), dst, ssem.at[j], rsem.at[z], device)
            pl.when(z != LOW + j)(copy.start)
            sent_if.append((z != LOW + j, copy))

    def from_owner(j, src, dst, ssem, rsem):
        copy = remote(src, dst(j), ssem.at[0], rsem.at[j], at_core)
        pl.when(z != LOW + j)(copy.wait_recv)

    def to_all(src, dst, ssem, rsem):
        copies = [remote(src(z_of(d)), dst, ssem.at[d], rsem.at[mine], at_z(d)) for d in FAR]

        @pl.when(is_owner)
        def _():
            for copy in copies:
                copy.start()

        sent_if.extend((is_owner, copy) for copy in copies)

    load_h = pltpu.make_async_copy(h_hbm, h_in, ls.at[2])
    load_w = pltpu.make_async_copy(w_hbm, wf, ls.at[1])
    load_cnt = pltpu.make_async_copy(cnt_hbm, cnt, ls.at[0])
    load_h.start()
    load_w.start()
    load_cnt.start()
    load_h.wait()
    hown[...] = h_in[...].astype(BF)
    pl.semaphore_wait(barrier, len(friends))

    got_a = send_z(lambda s: hown, lambda s: ha.at[s], as_, ar)
    ha[z] = hown[...]

    load_w.wait()
    w_all = wf[...]
    w_sum = jnp.sum(w_all, axis=0, keepdims=True)
    h_own = h_in[...]
    for j in range(4):
        for n in range(NC):
            base = n * CH + j * ZG
            fm[j, 2 * n : 2 * n + 2, :] = h_own[:, base : base + ZG]
        fm[j, 4:5, :] = jnp.concatenate([w_sum, w_sum], axis=1)
    to_owners(lambda j: fm.at[j], fr.at[z], fs, frs)
    fr[z] = fm[mine]
    w_copy = w_all.astype(BF)
    pick = (iota((128, 128), 0) == natural(iota((128, 128), 1))).astype(F32).astype(BF)
    pick_t = (natural(iota((128, 128), 0)) == iota((128, 128), 1)).astype(F32).astype(BF)
    wp[...] = jnp.dot(w_copy, pick, preferred_element_type=F32).astype(BF)
    wt[...] = lax.dot_general(
        pick_t, w_copy, (((1,), (1,)), ((), ())), preferred_element_type=F32
    ).astype(BF)

    for far, copies in ((0, got_a[0:3]), (1, got_a[3:7])):
        for copy in copies:
            copy.wait_recv()
        at = half * (1 - far) + (1 - half) * far
        for j in range(4):
            hx32[at, 2 * j : 2 * j + 2, :] = ha[at * 4 + j].astype(F32)
    hmat[slot] = hx32[...].reshape(16, 2048).astype(BF)

    def fan_out(buf, phase, n, cols):
        mine = buf.at[slot, :, cols]
        got_x = {d: send(mine, mine, xs.at[phase, n, d - 1], xr.at[phase, n, d - 1], at_x(d)) for d in (2, 1, 3)}
        got_c = [send(mine, mine, cs.at[phase, n, 0], cr.at[phase, n, 0], at_core)]
        return got_x, got_c

    def fan_on(buf, phase, n, cols, got):
        for d in (1, 3, 2):
            got[0][d].wait_recv()
            piece = buf.at[k * 4 + (x + 4 - d) % 4, :, cols]
            got[1].append(send(piece, piece, cs.at[phase, n, d], cr.at[phase, n, d], at_core))

    def fan_in(got):
        for copy in got[1]:
            copy.wait_recv()

    def quotients(n, first, last):
        cols = slice(n * CH, (n + 1) * CH)
        h_chunk = hmat[:, :, cols].reshape(128, CH)
        for i in range(first, last):
            rows = slice(i * 120, (i + 1) * 120)
            modeled = jnp.dot(wp[rows, :], h_chunk, preferred_element_type=F32)
            counts = cnt[rows, cols].astype(F32)
            quo[rows, :] = (counts * pltpu.reciprocal(modeled, approx=True)).astype(BF)

    def numerator(n):
        part = jnp.dot(wt[...], quo[...], preferred_element_type=F32)
        num[n, 0] = part[0:64, :]
        num[n, 1] = part[64:128, :]
        return send(num.at[n, 1 - k], numr.at[n], ns.at[n], nr.at[n], at_core)

    def sum_core(n, got):
        got.wait_recv()
        both = num[n, k] + numr[n]
        bs[n] = both.reshape(4, 16, CH)
        scale = scale_of(both)
        code = encode(both, scale)
        scale2 = twice(scale)
        for s in range(4):
            bx[n, s, :, 0:CH] = code[16 * s : 16 * s + 16, :]
            bx[n, s, :, CH : CH + 128] = scale2
        return {
            d: send(bx.at[n, (x + d) % 4], bxr.at[n, d - 1], bxs.at[n, d - 1], bxrs.at[n, d - 1], at_x(d))
            for d in (2, 1, 3)
        }

    def sum_x(n, got):
        total = bs[n, x]
        for d in (1, 3, 2):
            got[d].wait_recv()
            total = total + decode(bxr[n, d - 1, :, 0:CH], bxr[n, d - 1, :, CH : CH + 128])
        scale = scale_of(total)
        code = encode(total, scale)
        scale2 = twice(scale)
        for s in range(4):
            tz[n, s] = total[:, s * ZG : (s + 1) * ZG]
            bz[n, s, :, 0:ZG] = code[:, s * ZG : (s + 1) * ZG]
            bz[n, s, :, ZG : ZG + 128] = scale2
        to_owners(lambda j: bz.at[n, j], bzr.at[n, z], bzs.at[n], bzrs.at[n])

    def sum_z(n):
        places_z = [z_of(d) for d in NEAR]
        dues = [remote(bz.at[n, 0], bzr.at[n, s], bzs.at[n, 0], bzrs.at[n, s], at_core) for s in places_z]

        @pl.when(is_owner)
        def _():
            total = tz[n, mine]
            for s, copy in zip(places_z, dues):
                copy.wait_recv()
                total = total + decode(bzr[n, s, :, 0:ZG], bzr[n, s, :, ZG : ZG + 128])
            updated = h16[n] * total / w_column
            hu[n] = updated.astype(BF)
            hmat2[slot, :, genes(n, mine)] = hu[n]
            for zz in range(8):
                ho[n, zz] = updated[2 * zz : 2 * zz + 2, :]
            outr[:, genes(n, mine)] = ho[n, z]

        to_all(lambda s: hu.at[n], hmat2.at[slot, :, genes(n, mine)], cz.at[n], czr.at[n])

    got = [fan_out(hmat, 0, n, pl.ds(n * CH, CH)) for n in range(NC)]

    due_f = [remote(fm.at[0], fr.at[z_of(d)], fs.at[0], frs.at[z_of(d)], at_core) for d in NEAR]

    @pl.when(is_owner)
    def _():
        for copy in due_f:
            copy.wait_recv()

    tot = jnp.zeros((1, 128), F32)
    for zz in range(8):
        tot = tot + fr[zz, 4:5, 0:128]
        for n in range(NC):
            h16[n, 2 * zz : 2 * zz + 2, :] = fr[zz, 2 * n : 2 * n + 2, :]
    tx[x] = jnp.broadcast_to(tot, (8, 128))
    got_t = [send(tx.at[x], tx.at[x], txs.at[d - 1], txr.at[d - 1], at_x(d)) for d in (2, 1, 3)]
    load_cnt.wait()

    fan_on(hmat, 0, 0, pl.ds(0, CH), got[0])
    fan_on(hmat, 0, 1, pl.ds(CH, CH), got[1])
    got_n = []
    for n in range(NC):
        fan_in(got[n])
        quotients(n, 0, 8)
        got_n.append(numerator(n))
    got_bx = [sum_core(0, got_n[0])]
    for copy in got_t:
        copy.wait_recv()
    tc[k] = tx[0] + tx[1] + tx[2] + tx[3]
    got_tc = send(tc.at[k], tc.at[k], tcs.at[0], tcr.at[0], at_core)
    got_bx.append(sum_core(1, got_n[1]))
    got_tc.wait_recv()
    w_totals = tc[0][0:1, :] + tc[1][0:1, :]
    places = iota((16, 128), 0)
    own = (places // 2) * 16 + x * 4 + k * 2 + places % 2 == iota((16, 128), 1)
    w_column = jnp.sum(jnp.where(own, w_totals, 0.0), axis=1, keepdims=True)
    for n in range(NC):
        sum_x(n, got_bx[n])
    for n in range(NC):
        sum_z(n)

    def columns(piece):
        at = half if piece < 2 else 1 - half
        return pl.ds(pl.multiple_of((piece % 2) * CH + at * HALF, HALF), HALF)

    got = []

    def z_then_out(piece):
        n = piece % 2
        at = half if piece < 2 else 1 - half
        for i in range(2):
            from_owner(2 * at + i, hu.at[n], lambda j: hmat2.at[slot, :, genes(n, j)], cz.at[n], czr.at[n])
        got.append(fan_out(hmat2, 1, piece, columns(piece)))

    def pass_on(piece):
        fan_on(hmat2, 1, piece, columns(piece), got[piece])

    z_then_out(0)
    z_then_out(1)
    z_then_out(2)
    pass_on(0)
    z_then_out(3)
    pass_on(1)
    for n in range(NC):
        to_all(lambda s: ho.at[n, s], outr.at[:, genes(n, mine)], os_.at[n], ors.at[n])
    fan_in(got[0])
    fan_in(got[1])

    def h_natural(piece):
        cols = columns(piece)
        hn[:, cols] = jnp.dot(
            pick, hmat2[:, :, cols].reshape(128, HALF), preferred_element_type=F32
        ).astype(BF)

    def w_part(far, rows):
        acc = None
        for piece in (2 * far, 2 * far + 1):
            cols = columns(piece)
            modeled = jnp.dot(
                wp[rows, :], hmat2[:, :, cols].reshape(128, HALF), preferred_element_type=F32
            )
            counts = cnt[rows, cols].astype(F32)
            quotient = (counts * pltpu.reciprocal(modeled, approx=True)).astype(BF)
            term = lax.dot_general(
                quotient, hn[:, cols], (((1,), (1,)), ((), ())), preferred_element_type=F32
            )
            acc = term if acc is None else acc + term
        return acc

    h_natural(0)
    h_natural(1)
    for i in range(4):
        rows = slice(i * 240, (i + 1) * 240)
        wn[rows, :] = w_part(0, rows)
        if i == 1:
            pass_on(2)
    pass_on(3)
    fan_in(got[2])
    fan_in(got[3])
    h_natural(2)
    h_natural(3)

    def code_y(part, d, value):
        size = SIZES[part]
        scale = scale_of(value)
        dy[part, d - 1, 0:size, :] = encode(value, scale)
        dy[part, d - 1, size : size + 16, :] = twice(scale)
        whole = pl.ds(0, size + 16)
        return send(
            dy.at[part, d - 1, whole], dyr.at[part, d - 1, whole], dys.at[part, d - 1], dyrs.at[part, d - 1], at_y(d)
        )

    def rows_of(part, owner):
        return pl.ds(pl.multiple_of(owner * ROWS + STARTS[part], 16), SIZES[part])

    def sum_y(part, got):
        size = SIZES[part]
        total = wn[rows_of(part, y), :]
        for d in (1, 3, 2):
            got[d].wait_recv()
            total = total + decode(dyr[part, d - 1, 0:size, :], dyr[part, d - 1, size : size + 16, :])
        scale = scale_of(total)
        dz[part, 0:size, :] = encode(total, scale)
        dz[part, size : size + 16, :] = twice(scale)
        whole = pl.ds(0, size + 16)
        return send(dz.at[part, whole], zr.at[part, whole], dzs.at[part], dzr.at[part], at_zh)

    got_y = [{}, {}]
    got_z = []
    for part in range(2):
        for d in (2, 1, 3, 0):
            rows = rows_of(part, (y + d) % 4)
            value = wn[rows, :] + w_part(1, rows)
            if d:
                got_y[part][d] = code_y(part, d, value)
            else:
                wn[rows, :] = value
    ht[y] = lax.dot_general(
        jnp.ones((8, 2048), BF), hn[...], (((1,), (1,)), ((), ())), preferred_element_type=F32
    )
    got_h = [send(ht.at[y], ht.at[y], hts.at[d - 1], htr.at[d - 1], at_y(d)) for d in (2, 1, 3)]
    got_z += [sum_y(part, got_y[part]) for part in range(2)]
    for copy in got_h:
        copy.wait_recv()
    hz[zh] = ht[0] + ht[1] + ht[2] + ht[3]
    got_hz = send(hz.at[zh], hz.at[zh], hzs.at[0], hzr.at[0], at_zh)
    for n in range(NC):
        for j in range(4):
            from_owner(j, ho.at[n, 0], lambda j: outr.at[:, genes(n, j)], os_.at[n], ors.at[n])
    give_h = pltpu.make_async_copy(outr, h_out, ls.at[2])
    give_h.start()

    got_w = []
    for part in range(2):
        size = SIZES[part]
        got_z[part].wait_recv()
        total = decode(dz[part, 0:size, :], dz[part, size : size + 16, :])
        total = total + decode(zr[part, 0:size, :], zr[part, size : size + 16, :])
        scale = scale_of(total)
        da[part, y, 0:size, :] = encode(total, scale)
        da[part, y, size : size + 16, :] = twice(scale)
        code = da.at[part, y, pl.ds(0, size + 16)]
        got_w.append({d: send(code, code, das.at[part, d - 1], dar.at[part, d - 1], at_y(d)) for d in (2, 1, 3)})
    got_hz.wait_recv()
    h_totals = hz[0] + hz[1]
    gives = [give_h]
    for part in range(2):
        size = SIZES[part]
        inverse = spread(1.0 / h_totals, size, 128)
        for d in (0, 1, 3, 2):
            if d:
                got_w[part][d].wait_recv()
            p = (y + 4 - d) % 4
            rows = rows_of(part, p)
            share = decode(da[part, p, 0:size, :], da[part, p, size : size + 16, :])
            wv[rows, :] = wf[rows, :] * (share * inverse)
            given = pltpu.make_async_copy(wv.at[rows, :], w_out.at[rows, :], gs.at[part, d])
            given.start()
            gives.append(given)
    for copy in sent:
        copy.wait_send()
    for condition, copy in sent_if:
        pl.when(condition)(copy.wait_send)
    for given in gives:
        given.wait()


def hand_on(w_in, h_in, w_out, h_out, w_mid, h_mid, sems):
    moves = [(h_in, h_mid, h_out)]
    for i in range(4):
        rows = pl.ds(i * ROWS, ROWS)
        moves.append((w_in.at[rows, :], w_mid.at[rows, :], w_out.at[rows, :]))
    arrive = [pltpu.make_async_copy(src, mid, sems.at[0, i]) for i, (src, mid, dst) in enumerate(moves)]
    leave = [pltpu.make_async_copy(mid, dst, sems.at[1, i]) for i, (src, mid, dst) in enumerate(moves)]
    for copy in arrive:
        copy.start()
    for before, after in zip(arrive, leave):
        before.wait()
        after.start()
    for copy in leave:
        copy.wait()


def per_device(counts, w_factor, h_factor):
    vmem = pltpu.VMEM
    dma = pltpu.SemaphoreType.DMA
    far = pl.BlockSpec(memory_space=pl.ANY)
    shapes = (jax.ShapeDtypeStruct((960, 128), F32), jax.ShapeDtypeStruct((2, 2048), F32))
    results = pl.pallas_call(
        kernel,
        out_shape=shapes,
        in_specs=[far, far, far],
        out_specs=(far, far),
        scratch_shapes=[
            vmem((960, 2048), BF), vmem((960, 128), F32), vmem((2, 2048), F32), vmem((960, 128), BF), vmem((128, 960), BF),
            vmem((960, CH), BF),
            vmem((2, 2048), BF), vmem((8, 2, 2048), BF), vmem((2, 8, 2048), F32), vmem((8, 16, 2048), BF),
            vmem((4, 8, ZG), F32), vmem((8, 8, ZG), F32), vmem((NC, 16, ZG), F32),
            vmem((4, 8, 128), F32), vmem((2, 8, 128), F32),
            vmem((NC, 2, 64, CH), F32), vmem((NC, 64, CH), F32), vmem((NC, 4, 16, CH), F32),
            vmem((NC, 4, 16, CH + 128), BF), vmem((NC, 3, 16, CH + 128), BF),
            vmem((NC, 4, 16, ZG), F32), vmem((NC, 4, 16, ZG + 128), BF), vmem((NC, 8, 16, ZG + 128), BF),
            vmem((NC, 16, ZG), BF), vmem((NC, 8, 2, ZG), F32), vmem((2, 2048), F32),
            vmem((8, 16, 2048), BF), vmem((128, 2048), BF), vmem((4, 8, 128), F32), vmem((2, 8, 128), F32),
            vmem((960, 128), F32), vmem((2, 3, 144, 128), BF), vmem((2, 3, 144, 128), BF),
            vmem((2, 144, 128), BF), vmem((2, 144, 128), BF), vmem((2, 4, 144, 128), BF), vmem((960, 128), F32),
            dma((3,)), dma((8,)), dma((8,)), dma((8,)), dma((8,)), dma((3,)), dma((3,)), dma((1,)), dma((1,)),
            dma((2, 4, 3)), dma((2, 4, 3)), dma((2, 4, 4)), dma((2, 4, 4)), dma((NC,)), dma((NC,)),
            dma((NC, 3)), dma((NC, 3)), dma((NC, 8)), dma((NC, 8)), dma((NC, 8)), dma((NC, 8)),
            dma((NC, 8)), dma((NC, 8)), dma((3,)), dma((3,)), dma((1,)), dma((1,)),
            dma((2, 3)), dma((2, 3)), dma((2,)), dma((2,)), dma((2, 3)), dma((2, 3)), dma((2, 4)),
        ],
        compiler_params=pltpu.CompilerParams(
            collective_id=0, has_side_effects=True, vmem_limit_bytes=56 * 1024 * 1024
        ),
        name="nmf_update",
    )(counts, w_factor, h_factor)
    return pl.pallas_call(
        hand_on,
        out_shape=shapes,
        in_specs=[far, far],
        out_specs=(far, far),
        scratch_shapes=[vmem((960, 128), F32), vmem((2, 2048), F32), dma((2, 5))],
        name="hand_on",
    )(*results)


def solution(mesh):
    in_specs = (P("cell", "gene"), P("cell", None), P("cell", "gene"))
    out_specs = (P("cell", None), P("cell", "gene"))
    return jax.shard_map(
        per_device, mesh=mesh, in_specs=in_specs, out_specs=out_specs, check_vma=False
    )
```

```python
import jax
import jax.numpy as jnp
from jax import lax
from jax.experimental import pallas as pl
from jax.experimental.pallas import tpu as pltpu
from jax.sharding import PartitionSpec as P

MESH = pl.DeviceIdType.MESH
BF = jnp.bfloat16
F32 = jnp.float32
NC = 2
CH = 2048 // NC
OWNERS = 2
ZG = CH // OWNERS
LOW = 3
HALF = CH // 2
ROWS = 240
STARTS, SIZES = (0, 128), (128, 112)
NEAR = (1, 2, 3, 4, 5, 6, 7)
FAR = (7, 6, 5, 4, 3, 2, 1)


def iota(shape, dim):
    return lax.broadcasted_iota(jnp.int32, shape, dim)


def natural(i):
    return ((i % 16) // 2) * 16 + ((i // 16) % 4) * 4 + (i // 64) * 2 + i % 2


def spread(tile, rows, columns):
    wide = jnp.concatenate([tile] * (columns // 128), axis=1) if columns > 128 else tile
    return jnp.concatenate([wide] * (rows // 8), axis=0) if rows > 8 else wide


def scale_of(value):
    rows, columns = value.shape
    top = jnp.full((8, 128), 1e-30, F32)
    for r in range(0, rows, 8):
        for c in range(0, columns, 128):
            top = jnp.maximum(top, value[r : r + 8, c : c + 128])
    return top.astype(BF)


def encode(value, scale):
    rows, columns = value.shape
    share = value * spread(32768.0 / scale.astype(F32), rows, columns)
    square = share * share
    fourth = square * square
    return (fourth * fourth).astype(BF)


def decode(code, scale16):
    rows, columns = code.shape
    unit = scale16[0:8, :].astype(F32) * (1.0 / 32768.0)
    root = jnp.sqrt(jnp.sqrt(jnp.sqrt(code.astype(F32))))
    return root * spread(unit, rows, columns)


def twice(scale):
    wide = scale.astype(F32)
    return jnp.concatenate([wide, wide], axis=0).astype(BF)


def kernel(
    cnt_hbm, w_hbm, h_hbm, w_out, h_out,
    cnt, wf, h_in, wp, wt, quo,
    hown, ha, hx32, hmat, fm, fr, h16, tx, tc,
    num, numr, bs, bx, bxr, tz, bz, bzr, hu, ho, outr, hmat2, hn, ht, hz,
    wn, dy, dyr, dz, zr, da, wv,
    ls, as_, ar, fs, frs, txs, txr, tcs, tcr,
    xs, xr, cs, cr, ns, nr, bxs, bxrs, bzs, bzrs, cz, czr, os_, ors, hts, htr, hzs, hzr,
    dys, dyrs, dzs, dzr, das, dar, gs,
):
    c = lax.axis_index("cell")
    g = lax.axis_index("gene")
    z, x, k = c // 8, (c // 2) % 4, c % 2
    y, zh = g // 2, g % 2
    slot = k * 4 + x

    half = z // 4

    def z_of(d):
        return half * 4 + (z + d) % 4 if d < 4 else half * (7 - d) + (1 - half) * d

    def at_z(d):
        return (z_of(d) * 8 + x * 2 + k, g)

    def at_x(d):
        return (z * 8 + ((x + d) % 4) * 2 + k, g)

    def at_y(d):
        return (c, ((y + d) % 4) * 2 + zh)

    def genes(n, owner):
        return pl.ds(pl.multiple_of(n * CH + owner * ZG, ZG), ZG)

    at_core = (z * 8 + x * 2 + (1 - k), g)
    at_zh = (c, y * 2 + (1 - zh))
    sent = []

    def remote(src, dst, ssem, rsem, device):
        return pltpu.make_async_remote_copy(
            src_ref=src, dst_ref=dst, send_sem=ssem, recv_sem=rsem, device_id=device, device_id_type=MESH
        )

    def due(copy):
        return copy

    def send(src, dst, ssem, rsem, device):
        copy = remote(src, dst, ssem, rsem, device)
        copy.start()
        sent.append(copy)
        return due(copy)

    def send_z(src, dst, ssem, rsem):
        for d in FAR:
            copy = remote(src(z_of(d)), dst(z), ssem.at[d], rsem.at[z], at_z(d))
            copy.start()
            sent.append(copy)
        return [
            due(remote(src(z_of(d)), dst(z_of(d)), ssem.at[d], rsem.at[z_of(d)], at_z(d))) for d in NEAR
        ]

    barrier = pltpu.get_barrier_semaphore()
    friends = [at_z(d) for d in FAR] + [at_x(d) for d in range(1, 4)] + [at_core]
    friends += [at_y(d) for d in range(1, 4)] + [at_zh]
    for friend in friends:
        pl.semaphore_signal(barrier, inc=1, device_id=friend, device_id_type=MESH)

    is_owner = jnp.logical_and(z >= LOW, z < LOW + OWNERS)
    mine = jnp.clip(z - LOW, 0, OWNERS - 1)
    sent_if = []

    def to_owners(src, dst, ssem, rsem):
        for j in range(OWNERS):
            device = ((LOW + j) * 8 + x * 2 + k, g)
            copy = remote(src(j), dst, ssem.at[j], rsem.at[z], device)
            pl.when(z != LOW + j)(copy.start)
            sent_if.append((z != LOW + j, copy))

    def from_owner(j, src, dst, ssem, rsem):
        copy = remote(src, dst(j), ssem.at[0], rsem.at[j], at_core)
        pl.when(z != LOW + j)(copy.wait_recv)

    def to_all(src, dst, ssem, rsem):
        copies = [remote(src(z_of(d)), dst, ssem.at[d], rsem.at[mine], at_z(d)) for d in FAR]

        @pl.when(is_owner)
        def _():
            for copy in copies:
                copy.start()

        sent_if.extend((is_owner, copy) for copy in copies)

    load_h = pltpu.make_async_copy(h_hbm, h_in, ls.at[2])
    load_w = pltpu.make_async_copy(w_hbm, wf, ls.at[1])
    load_cnt = pltpu.make_async_copy(cnt_hbm, cnt, ls.at[0])
    load_h.start()
    load_w.start()
    load_cnt.start()
    load_h.wait()
    hown[...] = h_in[...].astype(BF)
    pl.semaphore_wait(barrier, len(friends))

    got_a = send_z(lambda s: hown, lambda s: ha.at[s], as_, ar)
    ha[z] = hown[...]

    load_w.wait()
    w_all = wf[...]
    w_sum = jnp.sum(w_all, axis=0, keepdims=True)
    h_own = h_in[...]
    for j in range(OWNERS):
        for n in range(NC):
            base = n * CH + j * ZG
            fm[j, 2 * n : 2 * n + 2, :] = h_own[:, base : base + ZG]
        fm[j, 4:5, :] = jnp.concatenate([w_sum] * (ZG // 128), axis=1)
    to_owners(lambda j: fm.at[j], fr.at[z], fs, frs)
    fr[z] = fm[mine]
    w_copy = w_all.astype(BF)
    pick = (iota((128, 128), 0) == natural(iota((128, 128), 1))).astype(F32).astype(BF)
    pick_t = (natural(iota((128, 128), 0)) == iota((128, 128), 1)).astype(F32).astype(BF)
    wp[...] = jnp.dot(w_copy, pick, preferred_element_type=F32).astype(BF)
    wt[...] = lax.dot_general(
        pick_t, w_copy, (((1,), (1,)), ((), ())), preferred_element_type=F32
    ).astype(BF)

    for far, copies in ((0, got_a[0:3]), (1, got_a[3:7])):
        for copy in copies:
            copy.wait_recv()
        at = half * (1 - far) + (1 - half) * far
        for j in range(4):
            hx32[at, 2 * j : 2 * j + 2, :] = ha[at * 4 + j].astype(F32)
    hmat[slot] = hx32[...].reshape(16, 2048).astype(BF)

    def fan_out(buf, phase, n, cols):
        mine = buf.at[slot, :, cols]
        got_x = {d: send(mine, mine, xs.at[phase, n, d - 1], xr.at[phase, n, d - 1], at_x(d)) for d in (2, 1, 3)}
        got_c = [send(mine, mine, cs.at[phase, n, 0], cr.at[phase, n, 0], at_core)]
        return got_x, got_c

    def fan_on(buf, phase, n, cols, got):
        for d in (1, 3, 2):
            got[0][d].wait_recv()
            piece = buf.at[k * 4 + (x + 4 - d) % 4, :, cols]
            got[1].append(send(piece, piece, cs.at[phase, n, d], cr.at[phase, n, d], at_core))

    def fan_in(got):
        for copy in got[1]:
            copy.wait_recv()

    def quotients(n, first, last):
        cols = slice(n * CH, (n + 1) * CH)
        h_chunk = hmat[:, :, cols].reshape(128, CH)
        for i in range(first, last):
            rows = slice(i * 120, (i + 1) * 120)
            modeled = jnp.dot(wp[rows, :], h_chunk, preferred_element_type=F32)
            counts = cnt[rows, cols].astype(F32)
            quo[rows, :] = (counts * pltpu.reciprocal(modeled, approx=True)).astype(BF)

    def numerator(n):
        part = jnp.dot(wt[...], quo[...], preferred_element_type=F32)
        num[n, 0] = part[0:64, :]
        num[n, 1] = part[64:128, :]
        return send(num.at[n, 1 - k], numr.at[n], ns.at[n], nr.at[n], at_core)

    def sum_core(n, got):
        got.wait_recv()
        both = num[n, k] + numr[n]
        bs[n] = both.reshape(4, 16, CH)
        scale = scale_of(both)
        code = encode(both, scale)
        scale2 = twice(scale)
        for s in range(4):
            bx[n, s, :, 0:CH] = code[16 * s : 16 * s + 16, :]
            bx[n, s, :, CH : CH + 128] = scale2
        return {
            d: send(bx.at[n, (x + d) % 4], bxr.at[n, d - 1], bxs.at[n, d - 1], bxrs.at[n, d - 1], at_x(d))
            for d in (2, 1, 3)
        }

    def sum_x(n, got):
        total = bs[n, x]
        for d in (1, 3, 2):
            got[d].wait_recv()
            total = total + decode(bxr[n, d - 1, :, 0:CH], bxr[n, d - 1, :, CH : CH + 128])
        scale = scale_of(total)
        code = encode(total, scale)
        scale2 = twice(scale)
        for s in range(OWNERS):
            tz[n, s] = total[:, s * ZG : (s + 1) * ZG]
            bz[n, s, :, 0:ZG] = code[:, s * ZG : (s + 1) * ZG]
            bz[n, s, :, ZG : ZG + 128] = scale2
        to_owners(lambda j: bz.at[n, j], bzr.at[n, z], bzs.at[n], bzrs.at[n])

    def sum_z(n):
        places_z = [z_of(d) for d in NEAR]
        dues = [remote(bz.at[n, 0], bzr.at[n, s], bzs.at[n, 0], bzrs.at[n, s], at_core) for s in places_z]

        @pl.when(is_owner)
        def _():
            total = tz[n, mine]
            for s, copy in zip(places_z, dues):
                copy.wait_recv()
                total = total + decode(bzr[n, s, :, 0:ZG], bzr[n, s, :, ZG : ZG + 128])
            updated = h16[n] * total / w_column
            hu[n] = updated.astype(BF)
            hmat2[slot, :, genes(n, mine)] = hu[n]
            for zz in range(8):
                ho[n, zz] = updated[2 * zz : 2 * zz + 2, :]
            outr[:, genes(n, mine)] = ho[n, z]

        to_all(lambda s: hu.at[n], hmat2.at[slot, :, genes(n, mine)], cz.at[n], czr.at[n])

    got = [fan_out(hmat, 0, n, pl.ds(n * CH, CH)) for n in range(NC)]

    due_f = [remote(fm.at[0], fr.at[z_of(d)], fs.at[0], frs.at[z_of(d)], at_core) for d in NEAR]

    @pl.when(is_owner)
    def _():
        for copy in due_f:
            copy.wait_recv()

    tot = jnp.zeros((1, 128), F32)
    for zz in range(8):
        tot = tot + fr[zz, 4:5, 0:128]
        for n in range(NC):
            h16[n, 2 * zz : 2 * zz + 2, :] = fr[zz, 2 * n : 2 * n + 2, :]
    tx[x] = jnp.broadcast_to(tot, (8, 128))
    got_t = [send(tx.at[x], tx.at[x], txs.at[d - 1], txr.at[d - 1], at_x(d)) for d in (2, 1, 3)]
    load_cnt.wait()

    fan_on(hmat, 0, 0, pl.ds(0, CH), got[0])
    fan_on(hmat, 0, 1, pl.ds(CH, CH), got[1])
    got_n = []
    for n in range(NC):
        fan_in(got[n])
        quotients(n, 0, 8)
        got_n.append(numerator(n))
    got_bx = [sum_core(0, got_n[0])]
    for copy in got_t:
        copy.wait_recv()
    tc[k] = tx[0] + tx[1] + tx[2] + tx[3]
    got_tc = send(tc.at[k], tc.at[k], tcs.at[0], tcr.at[0], at_core)
    got_bx.append(sum_core(1, got_n[1]))
    got_tc.wait_recv()
    w_totals = tc[0][0:1, :] + tc[1][0:1, :]
    places = iota((16, 128), 0)
    own = (places // 2) * 16 + x * 4 + k * 2 + places % 2 == iota((16, 128), 1)
    w_column = jnp.sum(jnp.where(own, w_totals, 0.0), axis=1, keepdims=True)
    for n in range(NC):
        sum_x(n, got_bx[n])
    for n in range(NC):
        sum_z(n)

    def columns(piece):
        at = half if piece < 2 else 1 - half
        return pl.ds(pl.multiple_of((piece % 2) * CH + at * HALF, HALF), HALF)

    got = []

    def z_then_out(piece):
        n = piece % 2
        at = half if piece < 2 else 1 - half
        for i in range(OWNERS // 2):
            from_owner(OWNERS // 2 * at + i, hu.at[n], lambda j: hmat2.at[slot, :, genes(n, j)], cz.at[n], czr.at[n])
        got.append(fan_out(hmat2, 1, piece, columns(piece)))

    def pass_on(piece):
        fan_on(hmat2, 1, piece, columns(piece), got[piece])

    z_then_out(0)
    z_then_out(1)
    z_then_out(2)
    pass_on(0)
    z_then_out(3)
    pass_on(1)
    for n in range(NC):
        to_all(lambda s: ho.at[n, s], outr.at[:, genes(n, mine)], os_.at[n], ors.at[n])
    fan_in(got[0])
    fan_in(got[1])

    def h_natural(piece):
        cols = columns(piece)
        hn[:, cols] = jnp.dot(
            pick, hmat2[:, :, cols].reshape(128, HALF), preferred_element_type=F32
        ).astype(BF)

    def w_part(far, rows):
        acc = None
        for piece in (2 * far, 2 * far + 1):
            cols = columns(piece)
            modeled = jnp.dot(
                wp[rows, :], hmat2[:, :, cols].reshape(128, HALF), preferred_element_type=F32
            )
            counts = cnt[rows, cols].astype(F32)
            quotient = (counts * pltpu.reciprocal(modeled, approx=True)).astype(BF)
            term = lax.dot_general(
                quotient, hn[:, cols], (((1,), (1,)), ((), ())), preferred_element_type=F32
            )
            acc = term if acc is None else acc + term
        return acc

    h_natural(0)
    h_natural(1)
    for i in range(4):
        rows = slice(i * 240, (i + 1) * 240)
        wn[rows, :] = w_part(0, rows)
        if i == 1:
            pass_on(2)
    pass_on(3)
    fan_in(got[2])
    fan_in(got[3])
    h_natural(2)
    h_natural(3)

    def code_y(part, d, value):
        size = SIZES[part]
        scale = scale_of(value)
        dy[part, d - 1, 0:size, :] = encode(value, scale)
        dy[part, d - 1, size : size + 16, :] = twice(scale)
        whole = pl.ds(0, size + 16)
        return send(
            dy.at[part, d - 1, whole], dyr.at[part, d - 1, whole], dys.at[part, d - 1], dyrs.at[part, d - 1], at_y(d)
        )

    def rows_of(part, owner):
        return pl.ds(pl.multiple_of(owner * ROWS + STARTS[part], 16), SIZES[part])

    def sum_y(part, got):
        size = SIZES[part]
        total = wn[rows_of(part, y), :]
        for d in (1, 3, 2):
            got[d].wait_recv()
            total = total + decode(dyr[part, d - 1, 0:size, :], dyr[part, d - 1, size : size + 16, :])
        scale = scale_of(total)
        dz[part, 0:size, :] = encode(total, scale)
        dz[part, size : size + 16, :] = twice(scale)
        whole = pl.ds(0, size + 16)
        return send(dz.at[part, whole], zr.at[part, whole], dzs.at[part], dzr.at[part], at_zh)

    got_y = [{}, {}]
    got_z = []
    for part in range(2):
        for d in (2, 1, 3, 0):
            rows = rows_of(part, (y + d) % 4)
            value = wn[rows, :] + w_part(1, rows)
            if d:
                got_y[part][d] = code_y(part, d, value)
            else:
                wn[rows, :] = value
    ht[y] = lax.dot_general(
        jnp.ones((8, 2048), BF), hn[...], (((1,), (1,)), ((), ())), preferred_element_type=F32
    )
    got_h = [send(ht.at[y], ht.at[y], hts.at[d - 1], htr.at[d - 1], at_y(d)) for d in (2, 1, 3)]
    got_z += [sum_y(part, got_y[part]) for part in range(2)]
    for copy in got_h:
        copy.wait_recv()
    hz[zh] = ht[0] + ht[1] + ht[2] + ht[3]
    got_hz = send(hz.at[zh], hz.at[zh], hzs.at[0], hzr.at[0], at_zh)
    for n in range(NC):
        for j in range(OWNERS):
            from_owner(j, ho.at[n, 0], lambda j: outr.at[:, genes(n, j)], os_.at[n], ors.at[n])
    give_h = pltpu.make_async_copy(outr, h_out, ls.at[2])
    give_h.start()

    got_w = []
    for part in range(2):
        size = SIZES[part]
        got_z[part].wait_recv()
        total = decode(dz[part, 0:size, :], dz[part, size : size + 16, :])
        total = total + decode(zr[part, 0:size, :], zr[part, size : size + 16, :])
        scale = scale_of(total)
        da[part, y, 0:size, :] = encode(total, scale)
        da[part, y, size : size + 16, :] = twice(scale)
        code = da.at[part, y, pl.ds(0, size + 16)]
        got_w.append({d: send(code, code, das.at[part, d - 1], dar.at[part, d - 1], at_y(d)) for d in (2, 1, 3)})
    got_hz.wait_recv()
    h_totals = hz[0] + hz[1]
    gives = [give_h]
    for part in range(2):
        size = SIZES[part]
        inverse = spread(1.0 / h_totals, size, 128)
        for d in (0, 1, 3, 2):
            if d:
                got_w[part][d].wait_recv()
            p = (y + 4 - d) % 4
            rows = rows_of(part, p)
            share = decode(da[part, p, 0:size, :], da[part, p, size : size + 16, :])
            wv[rows, :] = wf[rows, :] * (share * inverse)
            given = pltpu.make_async_copy(wv.at[rows, :], w_out.at[rows, :], gs.at[part, d])
            given.start()
            gives.append(given)
    for copy in sent:
        copy.wait_send()
    for condition, copy in sent_if:
        pl.when(condition)(copy.wait_send)
    for given in gives:
        given.wait()


def hand_on(w_in, h_in, w_out, h_out, w_mid, h_mid, sems):
    moves = [(h_in, h_mid, h_out)]
    for i in range(4):
        rows = pl.ds(i * ROWS, ROWS)
        moves.append((w_in.at[rows, :], w_mid.at[rows, :], w_out.at[rows, :]))
    arrive = [pltpu.make_async_copy(src, mid, sems.at[0, i]) for i, (src, mid, dst) in enumerate(moves)]
    leave = [pltpu.make_async_copy(mid, dst, sems.at[1, i]) for i, (src, mid, dst) in enumerate(moves)]
    for copy in arrive:
        copy.start()
    for before, after in zip(arrive, leave):
        before.wait()
        after.start()
    for copy in leave:
        copy.wait()


def per_device(counts, w_factor, h_factor):
    vmem = pltpu.VMEM
    dma = pltpu.SemaphoreType.DMA
    far = pl.BlockSpec(memory_space=pl.ANY)
    shapes = (jax.ShapeDtypeStruct((960, 128), F32), jax.ShapeDtypeStruct((2, 2048), F32))
    results = pl.pallas_call(
        kernel,
        out_shape=shapes,
        in_specs=[far, far, far],
        out_specs=(far, far),
        scratch_shapes=[
            vmem((960, 2048), BF), vmem((960, 128), F32), vmem((2, 2048), F32), vmem((960, 128), BF), vmem((128, 960), BF),
            vmem((960, CH), BF),
            vmem((2, 2048), BF), vmem((8, 2, 2048), BF), vmem((2, 8, 2048), F32), vmem((8, 16, 2048), BF),
            vmem((OWNERS, 8, ZG), F32), vmem((8, 8, ZG), F32), vmem((NC, 16, ZG), F32),
            vmem((4, 8, 128), F32), vmem((2, 8, 128), F32),
            vmem((NC, 2, 64, CH), F32), vmem((NC, 64, CH), F32), vmem((NC, 4, 16, CH), F32),
            vmem((NC, 4, 16, CH + 128), BF), vmem((NC, 3, 16, CH + 128), BF),
            vmem((NC, OWNERS, 16, ZG), F32), vmem((NC, OWNERS, 16, ZG + 128), BF), vmem((NC, 8, 16, ZG + 128), BF),
            vmem((NC, 16, ZG), BF), vmem((NC, 8, 2, ZG), F32), vmem((2, 2048), F32),
            vmem((8, 16, 2048), BF), vmem((128, 2048), BF), vmem((4, 8, 128), F32), vmem((2, 8, 128), F32),
            vmem((960, 128), F32), vmem((2, 3, 144, 128), BF), vmem((2, 3, 144, 128), BF),
            vmem((2, 144, 128), BF), vmem((2, 144, 128), BF), vmem((2, 4, 144, 128), BF), vmem((960, 128), F32),
            dma((3,)), dma((8,)), dma((8,)), dma((8,)), dma((8,)), dma((3,)), dma((3,)), dma((1,)), dma((1,)),
            dma((2, 4, 3)), dma((2, 4, 3)), dma((2, 4, 4)), dma((2, 4, 4)), dma((NC,)), dma((NC,)),
            dma((NC, 3)), dma((NC, 3)), dma((NC, 8)), dma((NC, 8)), dma((NC, 8)), dma((NC, 8)),
            dma((NC, 8)), dma((NC, 8)), dma((3,)), dma((3,)), dma((1,)), dma((1,)),
            dma((2, 3)), dma((2, 3)), dma((2,)), dma((2,)), dma((2, 3)), dma((2, 3)), dma((2, 4)),
        ],
        compiler_params=pltpu.CompilerParams(
            collective_id=0, has_side_effects=True, vmem_limit_bytes=56 * 1024 * 1024
        ),
        name="nmf_update",
    )(counts, w_factor, h_factor)
    return pl.pallas_call(
        hand_on,
        out_shape=shapes,
        in_specs=[far, far],
        out_specs=(far, far),
        scratch_shapes=[vmem((960, 128), F32), vmem((2, 2048), F32), dma((2, 5))],
        name="hand_on",
    )(*results)


def solution(mesh):
    in_specs = (P("cell", "gene"), P("cell", None), P("cell", "gene"))
    out_specs = (P("cell", None), P("cell", "gene"))
    return jax.shard_map(
        per_device, mesh=mesh, in_specs=in_specs, out_specs=out_specs, check_vma=False
    )
```

```python
import jax
import jax.numpy as jnp
from jax import lax
from jax.experimental import pallas as pl
from jax.experimental.pallas import tpu as pltpu
from jax.sharding import PartitionSpec as P

MESH = pl.DeviceIdType.MESH
BF = jnp.bfloat16
F32 = jnp.float32
NC = 2
CH = 2048 // NC
ZG = CH // 4
LOW = 2
HALF = CH // 2
ROWS = 240
STARTS, SIZES = (0, 128), (128, 112)
NEAR = (1, 2, 3, 4, 5, 6, 7)
FAR = (7, 6, 5, 4, 3, 2, 1)


def iota(shape, dim):
    return lax.broadcasted_iota(jnp.int32, shape, dim)


def natural(i):
    return ((i % 16) // 2) * 16 + ((i // 16) % 4) * 4 + (i // 64) * 2 + i % 2


def spread(tile, rows, columns):
    wide = jnp.concatenate([tile] * (columns // 128), axis=1) if columns > 128 else tile
    return jnp.concatenate([wide] * (rows // 8), axis=0) if rows > 8 else wide


def scale_of(value):
    rows, columns = value.shape
    top = jnp.full((8, 128), 1e-30, F32)
    for r in range(0, rows, 8):
        for c in range(0, columns, 128):
            top = jnp.maximum(top, value[r : r + 8, c : c + 128])
    return top.astype(BF)


def encode(value, scale):
    rows, columns = value.shape
    share = value * spread(32768.0 / scale.astype(F32), rows, columns)
    square = share * share
    fourth = square * square
    return (fourth * fourth).astype(BF)


def decode(code, scale16):
    rows, columns = code.shape
    unit = scale16[0:8, :].astype(F32) * (1.0 / 32768.0)
    root = jnp.sqrt(jnp.sqrt(jnp.sqrt(code.astype(F32))))
    return root * spread(unit, rows, columns)


def twice(scale):
    wide = scale.astype(F32)
    return jnp.concatenate([wide, wide], axis=0).astype(BF)


def kernel(
    cnt_hbm, w_hbm, h_hbm, w_out, h_out,
    cnt, wf, h_in, wp, wt, quo,
    hown, ha, hx32, hmat, fm, fr, h16, tx, tc,
    num, numr, bs, bx, bxr, tz, bz, bzr, hu, ho, outr, hmat2, hn, ht, hz,
    wn, dy, dyr, dz, zr, da, wv,
    ls, as_, ar, fs, frs, txs, txr, tcs, tcr,
    xs, xr, cs, cr, ns, nr, bxs, bxrs, bzs, bzrs, cz, czr, os_, ors, hts, htr, hzs, hzr,
    dys, dyrs, dzs, dzr, das, dar, gs,
):
    c = lax.axis_index("cell")
    g = lax.axis_index("gene")
    z, x, k = c // 8, (c // 2) % 4, c % 2
    y, zh = g // 2, g % 2
    slot = k * 4 + x

    half = z // 4

    def z_of(d):
        return half * 4 + (z + d) % 4 if d < 4 else half * (7 - d) + (1 - half) * d

    def at_z(d):
        return (z_of(d) * 8 + x * 2 + k, g)

    def at_x(d):
        return (z * 8 + ((x + d) % 4) * 2 + k, g)

    def at_y(d):
        return (c, ((y + d) % 4) * 2 + zh)

    def genes(n, owner):
        return pl.ds(pl.multiple_of(n * CH + owner * ZG, ZG), ZG)

    at_core = (z * 8 + x * 2 + (1 - k), g)
    at_zh = (c, y * 2 + (1 - zh))
    sent = []

    def remote(src, dst, ssem, rsem, device):
        return pltpu.make_async_remote_copy(
            src_ref=src, dst_ref=dst, send_sem=ssem, recv_sem=rsem, device_id=device, device_id_type=MESH
        )

    def due(copy):
        return copy

    def send(src, dst, ssem, rsem, device):
        copy = remote(src, dst, ssem, rsem, device)
        copy.start()
        sent.append(copy)
        return due(copy)

    def send_z(src, dst, ssem, rsem):
        for d in FAR:
            copy = remote(src(z_of(d)), dst(z), ssem.at[d], rsem.at[z], at_z(d))
            copy.start()
            sent.append(copy)
        return [
            due(remote(src(z_of(d)), dst(z_of(d)), ssem.at[d], rsem.at[z_of(d)], at_z(d))) for d in NEAR
        ]

    barrier = pltpu.get_barrier_semaphore()
    friends = [at_zh] + [at_z(d) for d in FAR] + [at_x(d) for d in range(1, 4)] + [at_core]
    friends += [at_y(d) for d in range(1, 4)]
    for friend in friends:
        pl.semaphore_signal(barrier, inc=1, device_id=friend, device_id_type=MESH)

    is_owner = jnp.logical_and(z >= LOW, z < LOW + 4)
    mine = jnp.clip(z - LOW, 0, 3)
    sent_if = []

    def to_owners(src, dst, ssem, rsem):
        for j in range(4):
            device = ((LOW + j) * 8 + x * 2 + k, g)
            copy = remote(src(j), dst, ssem.at[j], rsem.at[z], device)
            pl.when(z != LOW + j)(copy.start)
            sent_if.append((z != LOW + j, copy))

    def from_owner(j, src, dst, ssem, rsem):
        copy = remote(src, dst(j), ssem.at[0], rsem.at[j], at_core)
        pl.when(z != LOW + j)(copy.wait_recv)

    def to_all(src, dst, ssem, rsem):
        copies = [remote(src(z_of(d)), dst, ssem.at[d], rsem.at[mine], at_z(d)) for d in FAR]

        @pl.when(is_owner)
        def _():
            for copy in copies:
                copy.start()

        sent_if.extend((is_owner, copy) for copy in copies)

    load_h = pltpu.make_async_copy(h_hbm, h_in, ls.at[2])
    load_w = pltpu.make_async_copy(w_hbm, wf, ls.at[1])
    load_cnt = pltpu.make_async_copy(cnt_hbm, cnt, ls.at[0])
    load_h.start()
    load_w.start()
    load_cnt.start()
    load_h.wait()
    hown[...] = h_in[...].astype(BF)
    pl.semaphore_wait(barrier, len(friends))

    got_a = send_z(lambda s: hown, lambda s: ha.at[s], as_, ar)
    ha[z] = hown[...]

    load_w.wait()
    w_all = wf[...]
    w_sum = jnp.sum(w_all, axis=0, keepdims=True)
    h_own = h_in[...]
    for j in range(4):
        for n in range(NC):
            base = n * CH + j * ZG
            fm[j, 2 * n : 2 * n + 2, :] = h_own[:, base : base + ZG]
        fm[j, 4:5, :] = jnp.concatenate([w_sum, w_sum], axis=1)
    to_owners(lambda j: fm.at[j], fr.at[z], fs, frs)
    fr[z] = fm[mine]
    w_copy = w_all.astype(BF)
    pick = (iota((128, 128), 0) == natural(iota((128, 128), 1))).astype(F32).astype(BF)
    pick_t = (natural(iota((128, 128), 0)) == iota((128, 128), 1)).astype(F32).astype(BF)
    wp[...] = jnp.dot(w_copy, pick, preferred_element_type=F32).astype(BF)
    wt[...] = lax.dot_general(
        pick_t, w_copy, (((1,), (1,)), ((), ())), preferred_element_type=F32
    ).astype(BF)

    for far, copies in ((0, got_a[0:3]), (1, got_a[3:7])):
        for copy in copies:
            copy.wait_recv()
        at = half * (1 - far) + (1 - half) * far
        for j in range(4):
            hx32[at, 2 * j : 2 * j + 2, :] = ha[at * 4 + j].astype(F32)
    hmat[slot] = hx32[...].reshape(16, 2048).astype(BF)

    def fan_out(buf, phase, n, cols):
        mine = buf.at[slot, :, cols]
        got_x = {d: send(mine, mine, xs.at[phase, n, d - 1], xr.at[phase, n, d - 1], at_x(d)) for d in (2, 1, 3)}
        got_c = [send(mine, mine, cs.at[phase, n, 0], cr.at[phase, n, 0], at_core)]
        return got_x, got_c

    def fan_on(buf, phase, n, cols, got):
        for d in (1, 3, 2):
            got[0][d].wait_recv()
            piece = buf.at[k * 4 + (x + 4 - d) % 4, :, cols]
            got[1].append(send(piece, piece, cs.at[phase, n, d], cr.at[phase, n, d], at_core))

    def fan_in(got):
        for copy in got[1]:
            copy.wait_recv()

    def quotients(n, first, last):
        cols = slice(n * CH, (n + 1) * CH)
        h_chunk = hmat[:, :, cols].reshape(128, CH)
        for i in range(first, last):
            rows = slice(i * 120, (i + 1) * 120)
            modeled = jnp.dot(wp[rows, :], h_chunk, preferred_element_type=F32)
            counts = cnt[rows, cols].astype(F32)
            quo[rows, :] = (counts * pltpu.reciprocal(modeled, approx=True)).astype(BF)

    def numerator(n):
        part = jnp.dot(wt[...], quo[...], preferred_element_type=F32)
        num[n, 0] = part[0:64, :]
        num[n, 1] = part[64:128, :]
        return send(num.at[n, 1 - k], numr.at[n], ns.at[n], nr.at[n], at_core)

    def sum_core(n, got):
        got.wait_recv()
        both = num[n, k] + numr[n]
        bs[n] = both.reshape(4, 16, CH)
        scale = scale_of(both)
        code = encode(both, scale)
        scale2 = twice(scale)
        for s in range(4):
            bx[n, s, :, 0:CH] = code[16 * s : 16 * s + 16, :]
            bx[n, s, :, CH : CH + 128] = scale2
        return {
            d: send(bx.at[n, (x + d) % 4], bxr.at[n, d - 1], bxs.at[n, d - 1], bxrs.at[n, d - 1], at_x(d))
            for d in (2, 1, 3)
        }

    def sum_x(n, got):
        total = bs[n, x]
        for d in (1, 3, 2):
            got[d].wait_recv()
            total = total + decode(bxr[n, d - 1, :, 0:CH], bxr[n, d - 1, :, CH : CH + 128])
        scale = scale_of(total)
        code = encode(total, scale)
        scale2 = twice(scale)
        for s in range(4):
            tz[n, s] = total[:, s * ZG : (s + 1) * ZG]
            bz[n, s, :, 0:ZG] = code[:, s * ZG : (s + 1) * ZG]
            bz[n, s, :, ZG : ZG + 128] = scale2
        to_owners(lambda j: bz.at[n, j], bzr.at[n, z], bzs.at[n], bzrs.at[n])

    def sum_z(n):
        places_z = [z_of(d) for d in NEAR]
        dues = [remote(bz.at[n, 0], bzr.at[n, s], bzs.at[n, 0], bzrs.at[n, s], at_core) for s in places_z]

        @pl.when(is_owner)
        def _():
            total = tz[n, mine]
            for s, copy in zip(places_z, dues):
                copy.wait_recv()
                total = total + decode(bzr[n, s, :, 0:ZG], bzr[n, s, :, ZG : ZG + 128])
            updated = h16[n] * total / w_column
            hu[n] = updated.astype(BF)
            hmat2[slot, :, genes(n, mine)] = hu[n]
            for zz in range(8):
                ho[n, zz] = updated[2 * zz : 2 * zz + 2, :]
            outr[:, genes(n, mine)] = ho[n, z]

        to_all(lambda s: hu.at[n], hmat2.at[slot, :, genes(n, mine)], cz.at[n], czr.at[n])

    got = [fan_out(hmat, 0, n, pl.ds(n * CH, CH)) for n in range(NC)]

    due_f = [remote(fm.at[0], fr.at[z_of(d)], fs.at[0], frs.at[z_of(d)], at_core) for d in NEAR]

    @pl.when(is_owner)
    def _():
        for copy in due_f:
            copy.wait_recv()

    tot = jnp.zeros((1, 128), F32)
    for zz in range(8):
        tot = tot + fr[zz, 4:5, 0:128]
        for n in range(NC):
            h16[n, 2 * zz : 2 * zz + 2, :] = fr[zz, 2 * n : 2 * n + 2, :]
    tx[x] = jnp.broadcast_to(tot, (8, 128))
    got_t = [send(tx.at[x], tx.at[x], txs.at[d - 1], txr.at[d - 1], at_x(d)) for d in (2, 1, 3)]
    load_cnt.wait()

    fan_on(hmat, 0, 0, pl.ds(0, CH), got[0])
    fan_on(hmat, 0, 1, pl.ds(CH, CH), got[1])
    got_n = []
    for n in range(NC):
        fan_in(got[n])
        quotients(n, 0, 8)
        got_n.append(numerator(n))
    got_bx = [sum_core(0, got_n[0])]
    for copy in got_t:
        copy.wait_recv()
    tc[k] = tx[0] + tx[1] + tx[2] + tx[3]
    got_tc = send(tc.at[k], tc.at[k], tcs.at[0], tcr.at[0], at_core)
    got_bx.append(sum_core(1, got_n[1]))
    got_tc.wait_recv()
    w_totals = tc[0][0:1, :] + tc[1][0:1, :]
    places = iota((16, 128), 0)
    own = (places // 2) * 16 + x * 4 + k * 2 + places % 2 == iota((16, 128), 1)
    w_column = jnp.sum(jnp.where(own, w_totals, 0.0), axis=1, keepdims=True)
    for n in range(NC):
        sum_x(n, got_bx[n])
    for n in range(NC):
        sum_z(n)

    def columns(piece):
        at = half if piece < 2 else 1 - half
        return pl.ds(pl.multiple_of((piece % 2) * CH + at * HALF, HALF), HALF)

    got = []

    def z_then_out(piece):
        n = piece % 2
        at = half if piece < 2 else 1 - half
        for i in range(2):
            from_owner(2 * at + i, hu.at[n], lambda j: hmat2.at[slot, :, genes(n, j)], cz.at[n], czr.at[n])
        got.append(fan_out(hmat2, 1, piece, columns(piece)))

    def pass_on(piece):
        fan_on(hmat2, 1, piece, columns(piece), got[piece])

    z_then_out(0)
    z_then_out(1)
    z_then_out(2)
    pass_on(0)
    z_then_out(3)
    pass_on(1)
    for n in range(NC):
        to_all(lambda s: ho.at[n, s], outr.at[:, genes(n, mine)], os_.at[n], ors.at[n])
    fan_in(got[0])
    fan_in(got[1])

    def h_natural(piece):
        cols = columns(piece)
        hn[:, cols] = jnp.dot(
            pick, hmat2[:, :, cols].reshape(128, HALF), preferred_element_type=F32
        ).astype(BF)

    def w_part(far, rows):
        acc = None
        for piece in (2 * far, 2 * far + 1):
            cols = columns(piece)
            modeled = jnp.dot(
                wp[rows, :], hmat2[:, :, cols].reshape(128, HALF), preferred_element_type=F32
            )
            counts = cnt[rows, cols].astype(F32)
            quotient = (counts * pltpu.reciprocal(modeled, approx=True)).astype(BF)
            term = lax.dot_general(
                quotient, hn[:, cols], (((1,), (1,)), ((), ())), preferred_element_type=F32
            )
            acc = term if acc is None else acc + term
        return acc

    h_natural(0)
    h_natural(1)
    for i in range(4):
        rows = slice(i * 240, (i + 1) * 240)
        wn[rows, :] = w_part(0, rows)
        if i == 1:
            pass_on(2)
    pass_on(3)
    fan_in(got[2])
    fan_in(got[3])
    h_natural(2)
    h_natural(3)

    def code_y(part, d, value):
        size = SIZES[part]
        scale = scale_of(value)
        dy[part, d - 1, 0:size, :] = encode(value, scale)
        dy[part, d - 1, size : size + 16, :] = twice(scale)
        whole = pl.ds(0, size + 16)
        return send(
            dy.at[part, d - 1, whole], dyr.at[part, d - 1, whole], dys.at[part, d - 1], dyrs.at[part, d - 1], at_y(d)
        )

    def rows_of(part, owner):
        return pl.ds(pl.multiple_of(owner * ROWS + STARTS[part], 16), SIZES[part])

    def sum_y(part, got):
        size = SIZES[part]
        total = wn[rows_of(part, y), :]
        for d in (1, 3, 2):
            got[d].wait_recv()
            total = total + decode(dyr[part, d - 1, 0:size, :], dyr[part, d - 1, size : size + 16, :])
        scale = scale_of(total)
        dz[part, 0:size, :] = encode(total, scale)
        dz[part, size : size + 16, :] = twice(scale)
        whole = pl.ds(0, size + 16)
        return send(dz.at[part, whole], zr.at[part, whole], dzs.at[part], dzr.at[part], at_zh)

    got_y = [{}, {}]
    got_z = []
    for part in range(2):
        for d in (2, 1, 3, 0):
            rows = rows_of(part, (y + d) % 4)
            value = wn[rows, :] + w_part(1, rows)
            if d:
                got_y[part][d] = code_y(part, d, value)
            else:
                wn[rows, :] = value
    ht[y] = lax.dot_general(
        jnp.ones((8, 2048), BF), hn[...], (((1,), (1,)), ((), ())), preferred_element_type=F32
    )
    got_h = [send(ht.at[y], ht.at[y], hts.at[d - 1], htr.at[d - 1], at_y(d)) for d in (2, 1, 3)]
    early = list(sent)
    got_z += [sum_y(part, got_y[part]) for part in range(2)]
    for copy in got_h:
        copy.wait_recv()
    hz[zh] = ht[0] + ht[1] + ht[2] + ht[3]
    got_hz = send(hz.at[zh], hz.at[zh], hzs.at[0], hzr.at[0], at_zh)
    for n in range(NC):
        for j in range(4):
            from_owner(j, ho.at[n, 0], lambda j: outr.at[:, genes(n, j)], os_.at[n], ors.at[n])
    for copy in early:
        copy.wait_send()
    for condition, copy in sent_if:
        pl.when(condition)(copy.wait_send)
    give_h = pltpu.make_async_copy(outr, h_out, ls.at[2])
    give_h.start()

    got_w = []
    for part in range(2):
        size = SIZES[part]
        got_z[part].wait_recv()
        total = decode(dz[part, 0:size, :], dz[part, size : size + 16, :])
        total = total + decode(zr[part, 0:size, :], zr[part, size : size + 16, :])
        scale = scale_of(total)
        da[part, y, 0:size, :] = encode(total, scale)
        da[part, y, size : size + 16, :] = twice(scale)
        code = da.at[part, y, pl.ds(0, size + 16)]
        got_w.append({d: send(code, code, das.at[part, d - 1], dar.at[part, d - 1], at_y(d)) for d in (2, 1, 3)})
    got_hz.wait_recv()
    h_totals = hz[0] + hz[1]
    gives = [give_h]
    for part in range(2):
        size = SIZES[part]
        inverse = spread(1.0 / h_totals, size, 128)
        for d in (0, 1, 3, 2):
            if d:
                got_w[part][d].wait_recv()
            p = (y + 4 - d) % 4
            rows = rows_of(part, p)
            share = decode(da[part, p, 0:size, :], da[part, p, size : size + 16, :])
            wv[rows, :] = wf[rows, :] * (share * inverse)
            given = pltpu.make_async_copy(wv.at[rows, :], w_out.at[rows, :], gs.at[part, d])
            given.start()
            gives.append(given)
    for copy in sent[len(early) :]:
        copy.wait_send()
    for given in gives:
        given.wait()


def hand_on(w_in, h_in, w_out, h_out, w_mid, h_mid, sems):
    moves = [(h_in, h_mid, h_out)]
    for i in range(4):
        rows = pl.ds(i * ROWS, ROWS)
        moves.append((w_in.at[rows, :], w_mid.at[rows, :], w_out.at[rows, :]))
    arrive = [pltpu.make_async_copy(src, mid, sems.at[0, i]) for i, (src, mid, dst) in enumerate(moves)]
    leave = [pltpu.make_async_copy(mid, dst, sems.at[1, i]) for i, (src, mid, dst) in enumerate(moves)]
    for copy in arrive:
        copy.start()
    for before, after in zip(arrive, leave):
        before.wait()
        after.start()
    for copy in leave:
        copy.wait()


def per_device(counts, w_factor, h_factor):
    vmem = pltpu.VMEM
    dma = pltpu.SemaphoreType.DMA
    far = pl.BlockSpec(memory_space=pl.ANY)
    shapes = (jax.ShapeDtypeStruct((960, 128), F32), jax.ShapeDtypeStruct((2, 2048), F32))
    results = pl.pallas_call(
        kernel,
        out_shape=shapes,
        in_specs=[far, far, far],
        out_specs=(far, far),
        scratch_shapes=[
            vmem((960, 2048), BF), vmem((960, 128), F32), vmem((2, 2048), F32), vmem((960, 128), BF), vmem((128, 960), BF),
            vmem((960, CH), BF),
            vmem((2, 2048), BF), vmem((8, 2, 2048), BF), vmem((2, 8, 2048), F32), vmem((8, 16, 2048), BF),
            vmem((4, 8, ZG), F32), vmem((8, 8, ZG), F32), vmem((NC, 16, ZG), F32),
            vmem((4, 8, 128), F32), vmem((2, 8, 128), F32),
            vmem((NC, 2, 64, CH), F32), vmem((NC, 64, CH), F32), vmem((NC, 4, 16, CH), F32),
            vmem((NC, 4, 16, CH + 128), BF), vmem((NC, 3, 16, CH + 128), BF),
            vmem((NC, 4, 16, ZG), F32), vmem((NC, 4, 16, ZG + 128), BF), vmem((NC, 8, 16, ZG + 128), BF),
            vmem((NC, 16, ZG), BF), vmem((NC, 8, 2, ZG), F32), vmem((2, 2048), F32),
            vmem((8, 16, 2048), BF), vmem((128, 2048), BF), vmem((4, 8, 128), F32), vmem((2, 8, 128), F32),
            vmem((960, 128), F32), vmem((2, 3, 144, 128), BF), vmem((2, 3, 144, 128), BF),
            vmem((2, 144, 128), BF), vmem((2, 144, 128), BF), vmem((2, 4, 144, 128), BF), vmem((960, 128), F32),
            dma((3,)), dma((8,)), dma((8,)), dma((8,)), dma((8,)), dma((3,)), dma((3,)), dma((1,)), dma((1,)),
            dma((2, 4, 3)), dma((2, 4, 3)), dma((2, 4, 4)), dma((2, 4, 4)), dma((NC,)), dma((NC,)),
            dma((NC, 3)), dma((NC, 3)), dma((NC, 8)), dma((NC, 8)), dma((NC, 8)), dma((NC, 8)),
            dma((NC, 8)), dma((NC, 8)), dma((3,)), dma((3,)), dma((1,)), dma((1,)),
            dma((2, 3)), dma((2, 3)), dma((2,)), dma((2,)), dma((2, 3)), dma((2, 3)), dma((2, 4)),
        ],
        compiler_params=pltpu.CompilerParams(
            collective_id=0, has_side_effects=True, vmem_limit_bytes=56 * 1024 * 1024
        ),
        name="nmf_update",
    )(counts, w_factor, h_factor)
    return pl.pallas_call(
        hand_on,
        out_shape=shapes,
        in_specs=[far, far],
        out_specs=(far, far),
        scratch_shapes=[vmem((960, 128), F32), vmem((2, 2048), F32), dma((2, 5))],
        name="hand_on",
    )(*results)


def solution(mesh):
    in_specs = (P("cell", "gene"), P("cell", None), P("cell", "gene"))
    out_specs = (P("cell", None), P("cell", "gene"))
    return jax.shard_map(
        per_device, mesh=mesh, in_specs=in_specs, out_specs=out_specs, check_vma=False
    )
```
